256 devices in a mesh: sfc: 256 (over z, y, x, core).
Axes of the slice: x: 4, y: 4, z: 8, core: 2. Of those that a mesh axis runs over, the one named last changes fastest.
Arguments:
- b_tiles: bfloat16 [12288, 2, 128, 128], P('sfc'), may hold values from -0.5 to 0.5
- pressure_tile: int32 [12288, 2], P('sfc'), may hold values from 0 to 1535, as said below
- mobility: float32 [12288, 128], P('sfc'), may hold values from 0.1 to 10
- rhs: float32 [1536, 128], P('sfc'), may hold values from -6 to 6
Outputs:
- pressure: float32 [1536, 128], P('sfc')
The draws below stay inside these ranges and needn't reach their ends.
Inputs may be any that keep to these rules, and one draw needn't show every extreme that they name: `pressure_tile`: a velocity tile on the device with index d couples only with pressure tiles of device d or d + 1 (pressure tile t belongs to device t // 6); the 2 tiles of one velocity tile are distinct; local velocity tile j couples with local pressure tile j mod 6; the last device couples only with its own.
All inputs are finite; a program needn't handle non-finite values.
Results may differ from the reference program's by a relative error of at most 0.0012.
Values may be sent and summed in bfloat16 or wider, within the bound.
No kernel may reach another device: no remote copies, remote signals or barrier semaphores. Data moves between devices by JAX's collectives and lax.ppermute only.
A program may use at most 128 MiB of HBM per device.

```python
import math
import jax
import jax.numpy as jnp
from jax import lax

TB = 128
KP = 2
PT = 6
VT = 48
NPT = 1536
NVT = 12288
N_SFC = 256


def draw_pressure_tile(key, part):
    key = jax.random.fold_in(key, 7)
    width = 2 * PT
    row_ids = jnp.arange(NVT, dtype=jnp.int32)
    device = row_ids // VT
    local = row_ids % VT
    slots = jnp.arange(width, dtype=jnp.int32)
    scores = jax.random.randint(key, (NVT, width), 0, 65536, dtype=jnp.int32) * width + slots[None, :]
    own_slot = (local % PT)[:, None]
    scores = jnp.where(slots[None, :] == own_slot, scores + 16777216, scores)
    last = (device == N_SFC - 1)[:, None]
    scores = jnp.where(last & (slots[None, :] >= PT), scores - 16777216, scores)
    chosen = lax.top_k(scores, KP)[1].astype(jnp.int32)
    return (device[:, None] * PT + chosen).astype(jnp.int32)


def block_scale(stream_key, shape, shards, smallest, high):
    def one(dim, shards_of):
        draws = jax.random.uniform(jax.random.fold_in(jax.random.fold_in(stream_key, 6), dim), (shards_of,), jnp.float32, smallest / len(shards), high / len(shards))
        return jnp.repeat(jnp.exp(draws), shape[dim] // shards_of).reshape((-1,) + (1,) * (len(shape) - dim - 1))

    level = one(*shards[0])
    for cut in shards[1:]:
        level = level * one(*cut)
    return level


def normal_values(key, shape, scale, bound, split=(), kind=jnp.bfloat16):
    entries = jax.random.normal(key, shape, jnp.float32) * scale
    if len(split) > 0:
        entries = block_scale(key, shape, split, -0.22, 0.18) * entries
    return jnp.clip(entries, min=-bound, max=bound).astype(kind)


def setup_inputs(seed: int = 0) -> dict:
    key_list = jax.random.split(jax.random.key(seed), 5)
    b_tiles = normal_values(key_list[0], (NVT, KP, TB, TB), TB ** -0.5, 0.5, ((0, 256),))
    pressure_tile = draw_pressure_tile(jax.random.fold_in(key_list[4], 71), 0)
    mobility = jnp.clip(jnp.exp(math.log(10.0) - 4.6051702 * jax.random.uniform(key_list[2], (NVT, TB), jnp.float32) ** block_scale(key_list[2], (NVT, TB), ((0, 256),), -0.2, 0.2)), 0.1, 10.0)
    rhs = normal_values(key_list[3], (NPT, TB), 1.0, 6.0, ((0, 256),), jnp.float32)
    return {"b_tiles": b_tiles, "pressure_tile": pressure_tile, "mobility": mobility, "rhs": rhs}


relax = 0.5

def slot_grid(tiles, relative, weights, width):
    hp = lax.Precision.HIGHEST
    root = jnp.sqrt(weights)
    weighted = (tiles.astype(jnp.float32) * root[:, None, None, :]).astype(jnp.bfloat16)
    wide = weighted.astype(jnp.float32)
    prods = jnp.einsum('vkab,vlcb->vklac', wide, wide, precision=hp)
    onehot = (relative[:, :, None] == jnp.arange(width, dtype=jnp.int32)[None, None, :]).astype(jnp.float32)
    pairs = onehot[:, :, None, :, None] * onehot[:, None, :, None, :]
    grid = jnp.einsum('vklrs,vklac->rasc', pairs, prods, precision=hp)
    size = tiles.shape[2]
    return grid.reshape(width * size, width * size)

def reference(b_tiles, pressure_tile, mobility, rhs):
    rows = PT * TB

    def assemble(device):
        tiles = lax.dynamic_slice_in_dim(b_tiles, device * VT, VT, 0)
        relative = lax.dynamic_slice_in_dim(pressure_tile, device * VT, VT, 0) - device * PT
        weights = lax.dynamic_slice_in_dim(mobility, device * VT, VT, 0)
        grid = slot_grid(tiles, relative, weights, 2 * PT)
        return (grid[:rows, :rows], grid[:rows, rows:], grid[rows:, rows:])
    own, upper, corner = lax.map(assemble, jnp.arange(N_SFC, dtype=jnp.int32))
    blank = jnp.zeros((1, rows, rows), jnp.float32)
    centre = own + jnp.concatenate([blank, corner[:-1]], axis=0)
    lower = jnp.concatenate([blank, jnp.transpose(upper[:-1], (0, 2, 1))], axis=0)
    diagonal = jnp.diagonal(centre, axis1=1, axis2=2)
    hp = lax.Precision.HIGHEST

    def apply(values):
        edge = jnp.zeros((1, rows), jnp.float32)
        following = jnp.concatenate([values[1:], edge], axis=0)
        previous = jnp.concatenate([edge, values[:-1]], axis=0)
        result = jnp.einsum('eij,ej->ei', centre, values, precision=hp)
        result = result + jnp.einsum('eij,ej->ei', upper, following, precision=hp)
        return result + jnp.einsum('eij,ej->ei', lower, previous, precision=hp)
    target = rhs.reshape(N_SFC, rows)
    values = relax * target / diagonal
    for sweep in range(2):
        values = values + relax * (target - apply(values)) / diagonal
    return values.reshape(NPT, TB)
```

```python
import jax
import jax.numpy as jnp
from jax import lax
from jax.experimental import pallas as pl
from jax.experimental.pallas import tpu as pltpu
from jax.sharding import PartitionSpec as P

relax = 0.5
f32, bf16 = jnp.float32, jnp.bfloat16
UP = 8
CHUNKS = 6
VMEM = pl.BlockSpec(memory_space=pltpu.VMEM)
SMEM = pl.BlockSpec(memory_space=pltpu.SMEM)
ANY = pl.BlockSpec(memory_space=pl.ANY)
params = pltpu.CompilerParams(vmem_limit_bytes=32 * 1024 * 1024)


def table_row(tile, here):
    slot = tile - lax.axis_index("sfc") * here
    return jnp.where(slot >= here, slot - here + UP, slot)


def assemble(tiles, couples, mobility, rhs, weighted, own, up, sems):
    count, here = tiles.shape[0], rhs.shape[0]
    step = count // CHUNKS
    copies = []
    for c in range(CHUNKS):
        part = pl.ds(c * step, step)
        copies.append(pltpu.make_async_copy(tiles.at[part], weighted.at[part], sems.at[c]))
        copies[-1].start()
    sub = lax.broadcasted_iota(jnp.int32, (8, 128), 0)
    lane = lax.broadcasted_iota(jnp.int32, (8, 128), 1)
    rows = lax.broadcasted_iota(jnp.int32, (16, 128), 0)
    total = jnp.zeros((16, 128), f32)
    for c in range(CHUNKS):
        copies[c].wait()

        def body(j, total):
            v = c * step + j
            root = jnp.sqrt(mobility[pl.ds(v, 1), :])
            half = (weighted[v].astype(f32) * root).astype(bf16)
            weighted[v] = half
            for k in range(2):
                tile = half[k * 128 : (k + 1) * 128]
                square = lax.dot_general(
                    tile, tile, (((1,), (1,)), ((), ())), preferred_element_type=f32
                )
                picked = square[:8]
                for i in range(1, 16):
                    picked = jnp.where(lane // 8 == i, square[8 * i : 8 * i + 8], picked)
                picked = jnp.where(lane % 8 == sub, picked, 0.0)
                sums = jnp.sum(picked, axis=0, keepdims=True)
                row = table_row(couples[k, v], here)
                total = total + jnp.where(rows == row, sums, 0.0)
            return total

        total = lax.fori_loop(0, step, body, total, unroll=True)
    own[:8, :] = total[:8]
    own[8 : 8 + here, :] = rhs[...]
    up[...] = total[8:]


def multiply(weighted, couples, table, here, mine, following):
    for r in range(here):
        for base, values in ((0, mine), (UP, following)):
            wide = jnp.broadcast_to(values[r : r + 1], (8, 128))
            high = wide.astype(bf16).astype(f32)
            table[base + r] = jnp.concatenate([high, wide - high], axis=0).astype(bf16)
    rows = lax.broadcasted_iota(jnp.int32, (16, 128), 0)

    def body(v, total):
        half = weighted[v]
        first = table_row(couples[0, v], here)
        second = table_row(couples[1, v], here)
        left = jnp.concatenate([table[first], table[second]], axis=1)
        inner = jnp.dot(left, half, preferred_element_type=f32)
        inner = inner[:8] + inner[8:]
        high = inner.astype(bf16).astype(f32)
        left = jnp.concatenate([high, inner - high], axis=0).astype(bf16)
        outer = lax.dot_general(
            left, half, (((1,), (1,)), ((), ())), preferred_element_type=f32
        )
        outer = outer[:8] + outer[8:]
        for k, row in ((0, first), (1, second)):
            part = outer[:, k * 128 : (k + 1) * 128]
            total = total + jnp.where(rows == row, jnp.concatenate([part, part], axis=0), 0.0)
        return total

    return lax.fori_loop(0, weighted.shape[0], body, jnp.zeros((16, 128), f32), unroll=16)


def starts(here, own, up, from_prev, from_next):
    live = lax.broadcasted_iota(jnp.int32, (8, 128), 0) < here
    last = lax.axis_index("sfc") == lax.axis_size("sfc") - 1
    other = live & jnp.logical_not(last)
    diag = jnp.where(live, own[:8, :] + from_prev[...], 1.0)
    diag_next = jnp.where(other, from_next[:8, :] + up[...], 1.0)
    target = jnp.where(live, own[8:, :], 0.0)
    target_next = jnp.where(other, from_next[8:, :], 0.0)
    scale, scale_next = relax / diag, relax / diag_next
    return (scale, target, scale * target), (scale_next, target_next, scale_next * target_next)


def first_sweep(here, weighted, couples, own, up, from_prev, from_next, y_own, y_up, table):
    mine, following = starts(here, own, up, from_prev, from_next)
    total = multiply(weighted, couples, table, here, mine[2], following[2])
    y_own[...] = total[:8]
    y_up[...] = total[8:]


def second_sweep(here, weighted, couples, own, up, from_prev, from_next, y_own, y_up,
                 y_prev, y_next, z_up, rest, factor, table):
    (scale, target, p), (scale_next, target_next, p_next) = starts(here, own, up, from_prev, from_next)
    p = p + scale * (target - (y_own[...] + y_prev[...]))
    last = lax.axis_index("sfc") == lax.axis_size("sfc") - 1
    p_next = p_next + scale_next * (target_next - (y_next[...] + y_up[...]))
    p_next = jnp.where(last, 0.0, p_next)
    total = multiply(weighted, couples, table, here, p, p_next)
    z_up[...] = total[8:]
    rest[...] = p + scale * (target - total[:8])
    factor[...] = scale


def shift(block, distance):
    n = lax.axis_size("sfc")
    route = [(i, i + distance) for i in range(n) if 0 <= i + distance < n]
    return lax.ppermute(block, "sfc", route)


def shards(b_tiles, pressure_tile, mobility, rhs):
    count, pairs, size = b_tiles.shape[:3]
    here = rhs.shape[0]
    tiles = pltpu.with_memory_space_constraint(
        b_tiles.reshape(count, pairs * size, size), pltpu.HBM
    )
    couples = pressure_tile.T
    small = jax.ShapeDtypeStruct((8, size), f32)
    weighted, own, up = pl.pallas_call(
        assemble,
        out_shape=(pltpu.VMEM(tiles.shape, bf16), jax.ShapeDtypeStruct((16, size), f32), small),
        in_specs=[ANY, SMEM, VMEM, VMEM],
        out_specs=(VMEM, VMEM, VMEM),
        scratch_shapes=[pltpu.SemaphoreType.DMA((CHUNKS,))],
        compiler_params=params,
        name="assemble",
    )(tiles, couples, mobility, rhs)
    table = pltpu.VMEM((16, 16, size), bf16)
    from_prev, from_next = shift(up, 1), shift(own, -1)
    weighted = pltpu.with_memory_space_constraint(weighted, pltpu.VMEM)
    known = (weighted, couples, own, up, from_prev, from_next)
    y_own, y_up = pl.pallas_call(
        lambda *refs: first_sweep(here, *refs),
        out_shape=(small, small),
        in_specs=[VMEM, SMEM] + [VMEM] * 4,
        out_specs=(VMEM, VMEM),
        scratch_shapes=[table],
        compiler_params=params,
        name="first_sweep",
    )(*known)
    y_prev, y_next = shift(y_up, 1), shift(y_own, -1)
    z_up, rest, factor = pl.pallas_call(
        lambda *refs: second_sweep(here, *refs),
        out_shape=(small, small, small),
        in_specs=[VMEM, SMEM] + [VMEM] * 8,
        out_specs=(VMEM, VMEM, VMEM),
        scratch_shapes=[table],
        compiler_params=params,
        name="second_sweep",
    )(*known, y_own, y_up, y_prev, y_next)
    z_prev = shift(z_up, 1)
    return (rest - factor * z_prev)[:here]


def solution(mesh):
    placed = (P("sfc", None, None, None), P("sfc", None), P("sfc", None), P("sfc", None))
    return jax.shard_map(
        shards, mesh=mesh, in_specs=placed, out_specs=P("sfc", None), check_vma=False
    )
```

```python
import functools

import jax
import jax.numpy as jnp
from jax import lax
from jax.experimental import pallas as pl
from jax.experimental.pallas import tpu as pltpu
from jax.sharding import PartitionSpec as P

relax = 0.5
f32, bf16 = jnp.float32, jnp.bfloat16
UP = 8
CHUNKS = 6
GROUP = 8
ODD, EVEN = 1, 0
cost = pl.CostEstimate(flops=10**10, bytes_accessed=10**8, transcendentals=0)
VMEM = pl.BlockSpec(memory_space=pltpu.VMEM)
ANY = pl.BlockSpec(memory_space=pl.ANY)
params = pltpu.CompilerParams(vmem_limit_bytes=32 * 1024 * 1024)


def position():
    return lax.axis_index("sfc")


def is_last():
    return position() == lax.axis_size("sfc") - 1


def parts(values):
    high = values.astype(bf16).astype(f32)
    return high, values - high


def scatter(place, per_tile):
    total = None
    for k in range(2):
        high, rest = parts(per_tile[k])
        middle, low = parts(rest)
        wide = jnp.concatenate([high, middle, low], axis=1).astype(bf16)
        sums = jnp.dot(
            place[k][:, : wide.shape[0]].astype(bf16), wide, preferred_element_type=f32
        )
        size = sums.shape[1] // 3
        sums = sums[:, :size] + sums[:, size : 2 * size] + sums[:, 2 * size :]
        total = sums if total is None else total + sums
    return total


def assemble_here(tiles, couples, mobility, rhs, weighted, place, pick, own, up, scratch, sems):
    count, here = tiles.shape[0], rhs.shape[0]
    step = count // CHUNKS
    local_couples, local_mobility, local_rhs = scratch
    small = (couples, local_couples), (mobility, local_mobility), (rhs, local_rhs)
    small = [pltpu.make_async_copy(a, b, sems.at[CHUNKS + i]) for i, (a, b) in enumerate(small)]
    for copy in small:
        copy.start()
    copies = []
    for c in range(CHUNKS):
        part = pl.ds(c * step, step)
        copies.append(pltpu.make_async_copy(tiles.at[part], weighted.at[part], sems.at[c]))
        copies[-1].start()
    for copy in small:
        copy.wait()
    slot = local_couples[...] - position() * here
    slot = jnp.where(slot >= here, slot - here + UP, slot)
    rows = lax.broadcasted_iota(jnp.int32, (16, count), 0)
    places = [
        jnp.concatenate(
            [(rows == slot[k : k + 1]).astype(f32), jnp.zeros((16, 128 - count), f32)], axis=1
        )
        for k in range(2)
    ]
    for k in range(2):
        place[k] = places[k]
    pick[...] = jnp.concatenate(places + [jnp.zeros((96, 128), f32)], axis=0).T
    sub = lax.broadcasted_iota(jnp.int32, (8, 128), 0)
    lane = lax.broadcasted_iota(jnp.int32, (8, 128), 1)
    sums = [[], []]
    for c in range(CHUNKS):
        copies[c].wait()
        for g in range(step // GROUP):
            picked_rows = [jnp.zeros((8, 128), f32)] * 2
            for j in range(GROUP):
                v = c * step + g * GROUP + j
                root = jnp.sqrt(local_mobility[v : v + 1, :])
                half = (weighted[v].astype(f32) * root).astype(bf16)
                weighted[v] = half
                for k in range(2):
                    tile = half[k * 128 : (k + 1) * 128]
                    square = lax.dot_general(
                        tile, tile, (((1,), (1,)), ((), ())), preferred_element_type=f32
                    )
                    picked = square[:8]
                    for i in range(1, 16):
                        picked = jnp.where(lane // 8 == i, square[8 * i : 8 * i + 8], picked)
                    picked = jnp.where(lane % 8 == sub, picked, 0.0)
                    picked = jnp.sum(picked, axis=0, keepdims=True)
                    picked_rows[k] = jnp.where(sub == j, picked, picked_rows[k])
            for k in range(2):
                sums[k].append(picked_rows[k])
    total = scatter(places, [jnp.concatenate(s, axis=0) for s in sums])
    own[:8, :] = total[:8]
    own[8:, :] = jnp.concatenate([local_rhs[...], jnp.zeros((8 - here, 128), f32)], axis=0)
    up[...] = total[8:]


def assemble_odd(tiles, couples, mobility, rhs, weighted, place, pick, own, up, *scratch):
    @pl.when(position() % 2 == ODD)
    def _():
        assemble_here(
            tiles, couples, mobility, rhs, weighted, place, pick, own, up, scratch[:3], scratch[3]
        )

    @pl.when(position() % 2 == EVEN)
    def _():
        up[...] = jnp.zeros_like(up)


def assemble_even(tiles, couples, mobility, rhs, odd_own, odd_up,
                  weighted, place, pick, own, up, swapped, *scratch):
    @pl.when(position() % 2 == EVEN)
    def _():
        assemble_here(
            tiles, couples, mobility, rhs, weighted, place, pick, own, up, scratch[:3], scratch[3]
        )
        swapped[:8, :] = up[...]
        swapped[8:, :] = up[...]

    @pl.when(position() % 2 == ODD)
    def _():
        own[...] = jnp.zeros_like(own)
        swapped[...] = odd_own[...]


def pass_on(block, out):
    out[...] = block[...]


def multiply(weighted, place, pick, mine, following):
    count = weighted.shape[0]
    high, low = parts(jnp.concatenate([mine, following], axis=0))
    none = jnp.zeros_like(high)
    table = jnp.concatenate(
        [
            jnp.concatenate([high, none, low, none], axis=1),
            jnp.concatenate([none, high, none, low], axis=1),
        ],
        axis=0,
    ).astype(bf16)
    values = jnp.dot(pick[:count, :32].astype(bf16), table, preferred_element_type=f32)
    sub = lax.broadcasted_iota(jnp.int32, (8, 128), 0)
    sub2 = lax.broadcasted_iota(jnp.int32, (8, 256), 0)
    inner, outer = [], []
    for g in range(count // GROUP):
        block = values[GROUP * g : GROUP * (g + 1)]
        left = jnp.concatenate([block[:, :256], block[:, 256:]], axis=0).astype(bf16)
        total = None
        for j in range(0, GROUP, 2):
            v = GROUP * g + j
            right = jnp.concatenate([weighted[v], weighted[v + 1]], axis=1)
            both = jnp.dot(left, right, preferred_element_type=f32)
            both = both[:8] + both[8:]
            total = both[:, :128] if total is None else jnp.where(sub == j, both[:, :128], total)
            total = jnp.where(sub == j + 1, both[:, 128:], total)
        inner.append(total)
    for g in range(count // GROUP):
        left = jnp.concatenate(parts(inner[g]), axis=0).astype(bf16)
        total = None
        for j in range(GROUP):
            both = lax.dot_general(
                left, weighted[GROUP * g + j], (((1,), (1,)), ((), ())), preferred_element_type=f32
            )
            both = both[:8] + both[8:]
            total = both if total is None else jnp.where(sub2 == j, both, total)
        outer.append(total)
    outer = jnp.concatenate(outer, axis=0)
    total = scatter(place, [outer[:, :128], outer[:, 128:]])
    return total[:8], total[8:]


def starts(here, own, up, from_prev, from_next):
    live = lax.broadcasted_iota(jnp.int32, (8, 128), 0) < here
    other = live & jnp.logical_not(is_last())
    diag = jnp.where(live, own[:8, :] + from_prev[:8, :], 1.0)
    diag_next = jnp.where(other, from_next[:8, :] + up[...], 1.0)
    target = jnp.where(live, own[8:, :], 0.0)
    target_next = jnp.where(other, from_next[8:, :], 0.0)
    scale, scale_next = relax / diag, relax / diag_next
    return (scale, target, scale * target), (scale_next, target_next, scale_next * target_next)


def first_sweep(here, parity, weighted, place, pick, own, up, from_prev, from_next, *outs):
    y_own, y_up = outs[-2:]

    @pl.when(position() % 2 == parity)
    def _():
        mine, following = starts(here, own, up, from_prev, from_next)
        y_own[...], y_up[...] = multiply(weighted, place, pick, mine[2], following[2])

    @pl.when(position() % 2 != parity)
    def _():
        y_own[...] = y_up[...] = jnp.zeros_like(y_up)


def second_sweep(here, parity, weighted, place, pick, own, up, from_prev, from_next,
                 y_own, y_up, y_prev, y_next, *outs):
    z_up, rest, factor = outs[-3:]

    @pl.when(position() % 2 == parity)
    def _():
        mine, following = starts(here, own, up, from_prev, from_next)
        scale, target, p = mine
        scale_next, target_next, p_next = following
        p = p + scale * (target - (y_own[...] + y_prev[...]))
        p_next = p_next + scale_next * (target_next - (y_next[...] + y_up[...]))
        p_next = jnp.where(is_last(), 0.0, p_next)
        z_own, z_up[...] = multiply(weighted, place, pick, p, p_next)
        rest[...] = p + scale * (target - z_own)
        factor[...] = scale

    @pl.when(position() % 2 != parity)
    def _():
        z_up[...] = jnp.zeros_like(z_up)


def finish_even(rest, factor, z_prev, out):
    out[...] = rest[...] - factor[...] * z_prev[...]


def finish(even, rest, factor, z_prev, out):
    odd = rest[...] - factor[...] * z_prev[...]
    out[...] = jnp.where(position() % 2 == ODD, odd, even[...])[: out.shape[0]]


def to_next():
    n = lax.axis_size("sfc")
    plane = max(n // 8, 4)
    stops = [i + 4 for i in range(0, n - 4, plane) if i + 4 < n - 2]
    route = {i: i + 1 for i in range(n)}
    route.update(zip(stops + [n - 1], [0] + [i + 1 for i in stops]))
    return list(route.items())


def forward(block):
    return lax.ppermute(block, "sfc", to_next())


def backward(block):
    return lax.ppermute(block, "sfc", [(b, a) for a, b in to_next()])


def odd_to_next(block):
    n = lax.axis_size("sfc")
    return lax.ppermute(block, "sfc", [(i, i + 1) for i in range(ODD, n - 1, 2)])


def swap(block):
    return lax.ppermute(block, "sfc", [(i, i ^ 1) for i in range(lax.axis_size("sfc"))])


def shards(b_tiles, pressure_tile, mobility, rhs):
    count, pairs, size = b_tiles.shape[:3]
    here = rhs.shape[0]
    in_hbm = lambda a: pltpu.with_memory_space_constraint(a, pltpu.HBM)
    in_vmem = lambda a: pltpu.with_memory_space_constraint(a, pltpu.VMEM)
    tiles = b_tiles.reshape(count, pairs * size, size)
    args = tuple(in_hbm(a) for a in (tiles, pressure_tile.T, mobility, rhs))
    small = jax.ShapeDtypeStruct((8, size), f32)
    assembled = (
        pltpu.VMEM(tiles.shape, bf16),
        jax.ShapeDtypeStruct((2, 16, 128), f32),
        jax.ShapeDtypeStruct((128, 128), f32),
        jax.ShapeDtypeStruct((16, size), f32),
        small,
    )
    scratch = [
        pltpu.VMEM((pairs, count), jnp.int32),
        pltpu.VMEM((count, size), f32),
        pltpu.VMEM((here, size), f32),
        pltpu.SemaphoreType.DMA((CHUNKS + 3,)),
    ]

    def call(kernel, outs, name, *operands, **more):
        return pl.pallas_call(
            kernel,
            out_shape=outs,
            in_specs=[VMEM] * len(operands),
            out_specs=jax.tree.map(lambda _: VMEM, outs),
            compiler_params=params,
            cost_estimate=cost,
            name=name,
            **more,
        )(*operands)

    def assembled_by(kernel, outs, name, *order):
        weighted, *others = pl.pallas_call(
            kernel,
            out_shape=outs,
            in_specs=[ANY] * 4 + [VMEM] * len(order),
            out_specs=(VMEM,) * len(outs),
            scratch_shapes=scratch,
            compiler_params=params,
            cost_estimate=cost,
            name=name,
        )(*args, *order)
        return in_vmem(weighted), *others

    known_o = assembled_by(assemble_odd, assembled, "assemble_odd")
    up_e = odd_to_next(known_o[4])
    *known_e, swapped = assembled_by(
        assemble_even, assembled + assembled[3:4], "assemble_even", *known_o[3:]
    )
    next_own_o = backward(known_e[3])
    swapped = swap(swapped)
    up_e = call(pass_on, small, "pass_on", up_e)
    known_e = (*known_e, up_e, swapped)
    known_o = (*known_o, swapped, next_own_o)
    y_own_e, y_up_e = call(
        functools.partial(first_sweep, here, EVEN), (small, small), "first_even", *known_e
    )
    y_next_o = backward(y_own_e)
    y_prev_o = swap(y_up_e)
    y_own_o, y_up_o = call(
        functools.partial(first_sweep, here, ODD), (small, small), "first_odd", *known_o, y_up_e
    )
    y_prev_e = forward(y_up_o)
    y_next_e = swap(y_own_o)
    z_up_o, rest_o, factor_o = call(
        functools.partial(second_sweep, here, ODD), (small,) * 3, "second_odd",
        *known_o, y_own_o, y_up_o, y_prev_o, y_next_o,
    )
    z_prev_e = forward(z_up_o)
    z_up_e, rest_e, factor_e = call(
        functools.partial(second_sweep, here, EVEN), (small,) * 3, "second_even",
        *known_e, y_own_e, y_up_e, y_prev_e, y_next_e, z_up_o,
    )
    z_prev_o = swap(z_up_e)
    even = call(finish_even, small, "finish_even", rest_e, factor_e, z_prev_e)
    outs = jax.ShapeDtypeStruct(rhs.shape, f32)
    return call(finish, outs, "finish", even, rest_o, factor_o, z_prev_o)


def solution(mesh):
    placed = (P("sfc", None, None, None), P("sfc", None), P("sfc", None), P("sfc", None))
    return jax.shard_map(
        shards, mesh=mesh, in_specs=placed, out_specs=P("sfc", None), check_vma=False
    )
```

```python
import functools

import jax
import jax.numpy as jnp
from jax import lax
from jax.experimental import pallas as pl
from jax.experimental.pallas import tpu as pltpu
from jax.sharding import PartitionSpec as P

relax = 0.5
f32, bf16 = jnp.float32, jnp.bfloat16
UP = 8
CHUNKS = 6
GROUP = 8
ODD, EVEN = 1, 0
cost = pl.CostEstimate(flops=10**10, bytes_accessed=10**8, transcendentals=0)
VMEM = pl.BlockSpec(memory_space=pltpu.VMEM)
ANY = pl.BlockSpec(memory_space=pl.ANY)
params = pltpu.CompilerParams(vmem_limit_bytes=32 * 1024 * 1024)


def position():
    return lax.axis_index("sfc")


def is_last():
    return position() == lax.axis_size("sfc") - 1


def parts(values):
    high = values.astype(bf16).astype(f32)
    return high, values - high


def scatter(place, per_tile):
    total = None
    for k in range(2):
        high, rest = parts(per_tile[k])
        middle, low = parts(rest)
        wide = jnp.concatenate([high, middle, low], axis=1).astype(bf16)
        sums = jnp.dot(
            place[k][:, : wide.shape[0]].astype(bf16), wide, preferred_element_type=f32
        )
        size = sums.shape[1] // 3
        sums = sums[:, :size] + sums[:, size : 2 * size] + sums[:, 2 * size :]
        total = sums if total is None else total + sums
    return total


def assemble_here(tiles, couples, mobility, rhs, weighted, turned, place, pick, own, up,
                  local_couples, local_mobility, local_rhs, sems):
    count, here = tiles.shape[0], rhs.shape[0]
    step = count // CHUNKS
    small = (couples, local_couples), (mobility, local_mobility), (rhs, local_rhs)
    small = [pltpu.make_async_copy(a, b, sems.at[CHUNKS + i]) for i, (a, b) in enumerate(small)]
    for copy in small:
        copy.start()
    copies = []
    for c in range(CHUNKS):
        part = pl.ds(c * step, step)
        copies.append(pltpu.make_async_copy(tiles.at[part], weighted.at[part], sems.at[c]))
        copies[-1].start()
    for copy in small:
        copy.wait()
    slot = local_couples[...] - position() * here
    slot = jnp.where(slot >= here, slot - here + UP, slot)
    rows = lax.broadcasted_iota(jnp.int32, (16, count), 0)
    places = [
        jnp.concatenate(
            [(rows == slot[k : k + 1]).astype(f32), jnp.zeros((16, 128 - count), f32)], axis=1
        )
        for k in range(2)
    ]
    for k in range(2):
        place[k] = places[k]
    pick[...] = jnp.concatenate(places + [jnp.zeros((96, 128), f32)], axis=0).T
    local_mobility[...] = jnp.sqrt(local_mobility[...])
    sub = lax.broadcasted_iota(jnp.int32, (8, 256), 0)
    sums = []
    for c in range(CHUNKS):
        copies[c].wait()
        for v in range(c * step, (c + 1) * step):
            half = (weighted[v].astype(f32) * local_mobility[v : v + 1, :]).astype(bf16)
            weighted[v] = half
            half = half.T
            turned[v] = half
            square = half.astype(f32)
            square = square * square
            total = square[:8]
            for i in range(1, 16):
                total = total + square[8 * i : 8 * i + 8]
            total = jnp.sum(total, axis=0, keepdims=True)
            if v % GROUP == 0:
                sums.append(jnp.broadcast_to(total, (8, 256)))
            else:
                sums[-1] = jnp.where(sub == v % GROUP, total, sums[-1])
    sums = jnp.concatenate(sums, axis=0)
    total = scatter(places, [sums[:, :128], sums[:, 128:]])
    own[:8, :] = total[:8]
    own[8:, :] = jnp.concatenate([local_rhs[...], jnp.zeros((8 - here, 128), f32)], axis=0)
    up[...] = total[8:]


def assemble_odd(tiles, couples, mobility, rhs, weighted, turned, place, pick, own, up, *scratch):
    @pl.when(position() % 2 == ODD)
    def _():
        assemble_here(
            tiles, couples, mobility, rhs, weighted, turned, place, pick, own, up, *scratch
        )

    @pl.when(position() % 2 == EVEN)
    def _():
        up[...] = jnp.zeros_like(up)


def assemble_even(tiles, couples, mobility, rhs, odd_own, odd_up,
                  weighted, turned, place, pick, own, up, swapped, *scratch):
    @pl.when(position() % 2 == EVEN)
    def _():
        assemble_here(
            tiles, couples, mobility, rhs, weighted, turned, place, pick, own, up, *scratch
        )
        swapped[:8, :] = up[...]
        swapped[8:, :] = up[...]

    @pl.when(position() % 2 == ODD)
    def _():
        own[...] = jnp.zeros_like(own)
        swapped[...] = odd_own[...]


def pass_on(block, out):
    out[...] = block[...]


def multiply(weighted, turned, place, pick, mine, following):
    count = weighted.shape[0]
    high, low = parts(jnp.concatenate([mine, following], axis=0))
    none = jnp.zeros_like(high)
    table = jnp.concatenate(
        [
            jnp.concatenate([high, none, low, none], axis=1),
            jnp.concatenate([none, high, none, low], axis=1),
        ],
        axis=0,
    ).astype(bf16)
    values = jnp.dot(pick[:count, :32].astype(bf16), table, preferred_element_type=f32)
    sub = lax.broadcasted_iota(jnp.int32, (8, 128), 0)
    sub2 = lax.broadcasted_iota(jnp.int32, (8, 256), 0)
    inner, outer = [], []
    for g in range(count // GROUP):
        block = values[GROUP * g : GROUP * (g + 1)]
        left = jnp.concatenate([block[:, :256], block[:, 256:]], axis=0).astype(bf16)
        total = None
        for j in range(0, GROUP, 2):
            v = GROUP * g + j
            right = jnp.concatenate([weighted[v], weighted[v + 1]], axis=1)
            both = jnp.dot(left, right, preferred_element_type=f32)
            both = both[:8] + both[8:]
            total = both[:, :128] if total is None else jnp.where(sub == j, both[:, :128], total)
            total = jnp.where(sub == j + 1, both[:, 128:], total)
        inner.append(total)
    for g in range(count // GROUP):
        left = jnp.concatenate(parts(inner[g]), axis=0).astype(bf16)
        total = None
        for j in range(GROUP):
            both = jnp.dot(left, turned[GROUP * g + j], preferred_element_type=f32)
            both = both[:8] + both[8:]
            total = both if total is None else jnp.where(sub2 == j, both, total)
        outer.append(total)
    outer = jnp.concatenate(outer, axis=0)
    total = scatter(place, [outer[:, :128], outer[:, 128:]])
    return total[:8], total[8:]


def starts(here, own, up, from_prev, from_next):
    live = lax.broadcasted_iota(jnp.int32, (8, 128), 0) < here
    other = live & jnp.logical_not(is_last())
    diag = jnp.where(live, own[:8, :] + from_prev[:8, :], 1.0)
    diag_next = jnp.where(other, from_next[:8, :] + up[...], 1.0)
    target = jnp.where(live, own[8:, :], 0.0)
    target_next = jnp.where(other, from_next[8:, :], 0.0)
    scale, scale_next = relax / diag, relax / diag_next
    return scale, target, scale * target, scale_next, target_next, scale_next * target_next


def first_sweep(here, parity, weighted, turned, place, pick, own, up, from_prev, from_next, *outs):
    y_own, y_up, state = outs[-3:]

    @pl.when(position() % 2 == parity)
    def _():
        now = starts(here, own, up, from_prev, from_next)
        y_own[...], y_up[...] = multiply(weighted, turned, place, pick, now[2], now[5])
        for i in range(6):
            state[i] = now[i]

    @pl.when(position() % 2 != parity)
    def _():
        y_own[...] = y_up[...] = jnp.zeros_like(y_up)


def second_sweep(parity, weighted, turned, place, pick, y_own, y_up, state, y_prev, y_next, *outs):
    z_up, rest, factor = outs[-3:]

    @pl.when(position() % 2 == parity)
    def _():
        scale, target, p, scale_next, target_next, p_next = [state[i] for i in range(6)]
        p = p + scale * (target - (y_own[...] + y_prev[...]))
        p_next = p_next + scale_next * (target_next - (y_next[...] + y_up[...]))
        p_next = jnp.where(is_last(), 0.0, p_next)
        z_own, z_up[...] = multiply(weighted, turned, place, pick, p, p_next)
        rest[...] = p + scale * (target - z_own)
        factor[...] = scale

    @pl.when(position() % 2 != parity)
    def _():
        z_up[...] = jnp.zeros_like(z_up)


def finish_even(rest, factor, z_prev, out):
    out[...] = rest[...] - factor[...] * z_prev[...]


def finish(even, rest, factor, z_prev, out):
    odd = rest[...] - factor[...] * z_prev[...]
    out[...] = jnp.where(position() % 2 == ODD, odd, even[...])[: out.shape[0]]


def to_next():
    n = lax.axis_size("sfc")
    plane = max(n // 8, 4)
    stops = [i + 4 for i in range(0, n - 4, plane) if i + 4 < n - 2]
    route = {i: i + 1 for i in range(n)}
    route.update(zip(stops + [n - 1], [0] + [i + 1 for i in stops]))
    return list(route.items())


def forward(block):
    return lax.ppermute(block, "sfc", to_next())


def backward(block):
    return lax.ppermute(block, "sfc", [(b, a) for a, b in to_next()])


def odd_to_next(block):
    n = lax.axis_size("sfc")
    return lax.ppermute(block, "sfc", [(i, i + 1) for i in range(ODD, n - 1, 2)])


def swap(block):
    return lax.ppermute(block, "sfc", [(i, i ^ 1) for i in range(lax.axis_size("sfc"))])


def shards(b_tiles, pressure_tile, mobility, rhs):
    count, pairs, size = b_tiles.shape[:3]
    here = rhs.shape[0]
    in_hbm = lambda a: pltpu.with_memory_space_constraint(a, pltpu.HBM)
    in_vmem = lambda a: pltpu.with_memory_space_constraint(a, pltpu.VMEM)
    tiles = b_tiles.reshape(count, pairs * size, size)
    args = tuple(in_hbm(a) for a in (tiles, pressure_tile.T, mobility, rhs))
    small = jax.ShapeDtypeStruct((8, size), f32)
    assembled = (
        pltpu.VMEM(tiles.shape, bf16),
        pltpu.VMEM((count, size, pairs * size), bf16),
        jax.ShapeDtypeStruct((2, 16, 128), f32),
        jax.ShapeDtypeStruct((128, 128), f32),
        jax.ShapeDtypeStruct((16, size), f32),
        small,
    )
    scratch = [
        pltpu.VMEM((pairs, count), jnp.int32),
        pltpu.VMEM((count, size), f32),
        pltpu.VMEM((here, size), f32),
        pltpu.SemaphoreType.DMA((CHUNKS + 3,)),
    ]

    def call(kernel, outs, name, *operands, **more):
        return pl.pallas_call(
            kernel,
            out_shape=outs,
            in_specs=[VMEM] * len(operands),
            out_specs=jax.tree.map(lambda _: VMEM, outs),
            compiler_params=params,
            cost_estimate=cost,
            name=name,
            **more,
        )(*operands)

    def assembled_by(kernel, outs, name, *order):
        weighted, turned, *others = pl.pallas_call(
            kernel,
            out_shape=outs,
            in_specs=[ANY] * 4 + [VMEM] * len(order),
            out_specs=(VMEM,) * len(outs),
            scratch_shapes=scratch,
            compiler_params=params,
            cost_estimate=cost,
            name=name,
        )(*args, *order)
        return in_vmem(weighted), in_vmem(turned), *others

    *matrix_o, own_o, up_o = assembled_by(assemble_odd, assembled, "assemble_odd")
    from_prev_e = odd_to_next(up_o)
    *matrix_e, own_e, up_e, swapped = assembled_by(
        assemble_even, assembled + assembled[4:5], "assemble_even", own_o, up_o
    )
    from_next_o = backward(own_e)
    swapped = swap(swapped)
    from_prev_e = call(pass_on, small, "pass_on", from_prev_e)
    first = (small, small, jax.ShapeDtypeStruct((6, 8, size), f32))
    sweep_e = call(
        functools.partial(first_sweep, here, EVEN), first, "first_even",
        *matrix_e, own_e, up_e, from_prev_e, swapped,
    )
    y_next_o, y_prev_o = backward(sweep_e[0]), swap(sweep_e[1])
    sweep_o = call(
        functools.partial(first_sweep, here, ODD), first, "first_odd",
        *matrix_o, own_o, up_o, swapped, from_next_o, sweep_e[1],
    )
    y_prev_e, y_next_e = forward(sweep_o[1]), swap(sweep_o[0])
    z_up_o, rest_o, factor_o = call(
        functools.partial(second_sweep, ODD), (small,) * 3, "second_odd",
        *matrix_o, *sweep_o, y_prev_o, y_next_o,
    )
    z_prev_e = forward(z_up_o)
    z_up_e, rest_e, factor_e = call(
        functools.partial(second_sweep, EVEN), (small,) * 3, "second_even",
        *matrix_e, *sweep_e, y_prev_e, y_next_e, z_up_o,
    )
    z_prev_o = swap(z_up_e)
    even = call(finish_even, small, "finish_even", rest_e, factor_e, z_prev_e)
    outs = jax.ShapeDtypeStruct(rhs.shape, f32)
    return call(finish, outs, "finish", even, rest_o, factor_o, z_prev_o)


def solution(mesh):
    placed = (P("sfc", None, None, None), P("sfc", None), P("sfc", None), P("sfc", None))
    return jax.shard_map(
        shards, mesh=mesh, in_specs=placed, out_specs=P("sfc", None), check_vma=False
    )
```

```python
import functools

import jax
import jax.numpy as jnp
from jax import lax
from jax.experimental import pallas as pl
from jax.experimental.pallas import tpu as pltpu
from jax.sharding import PartitionSpec as P

relax = 0.5
f32, bf16 = jnp.float32, jnp.bfloat16
UP = 8
CHUNKS = 6
GROUP = 8
ODD, EVEN = 1, 0
cost = pl.CostEstimate(flops=10**10, bytes_accessed=10**8, transcendentals=0)
VMEM = pl.BlockSpec(memory_space=pltpu.VMEM)
ANY = pl.BlockSpec(memory_space=pl.ANY)
params = pltpu.CompilerParams(vmem_limit_bytes=32 * 1024 * 1024)


def position():
    return lax.axis_index("sfc")


def is_last():
    return position() == lax.axis_size("sfc") - 1


def plane_size():
    return max(lax.axis_size("sfc") // 8, 8)


def is_tail():
    size = plane_size()
    return (position() % size == size - 1) & jnp.logical_not(is_last())


def is_head():
    return position() % plane_size() == 0


def parts(values):
    high = values.astype(bf16).astype(f32)
    return high, values - high


def scatter(place, per_tile):
    total = None
    for k in range(2):
        high, rest = parts(per_tile[k])
        middle, low = parts(rest)
        wide = jnp.concatenate([high, middle, low], axis=1).astype(bf16)
        sums = jnp.dot(
            place[k][:, : wide.shape[0]].astype(bf16), wide, preferred_element_type=f32
        )
        size = sums.shape[1] // 3
        sums = sums[:, :size] + sums[:, size : 2 * size] + sums[:, 2 * size :]
        total = sums if total is None else total + sums
    return total


def assemble_here(tiles, couples, mobility, rhs, weighted, turned, place, pick, own, up,
                  local_couples, local_mobility, local_rhs, sems):
    count, here = tiles.shape[0], rhs.shape[0]
    step = count // CHUNKS
    small = (couples, local_couples), (mobility, local_mobility), (rhs, local_rhs)
    small = [pltpu.make_async_copy(a, b, sems.at[CHUNKS + i]) for i, (a, b) in enumerate(small)]
    for copy in small:
        copy.start()
    copies = []
    for c in range(CHUNKS):
        part = pl.ds(c * step, step)
        copies.append(pltpu.make_async_copy(tiles.at[part], weighted.at[part], sems.at[c]))
        copies[-1].start()
    for copy in small:
        copy.wait()
    slot = local_couples[...] - position() * here
    slot = jnp.where(slot >= here, slot - here + UP, slot)
    rows = lax.broadcasted_iota(jnp.int32, (16, count), 0)
    places = [
        jnp.concatenate(
            [(rows == slot[k : k + 1]).astype(f32), jnp.zeros((16, 128 - count), f32)], axis=1
        )
        for k in range(2)
    ]
    for k in range(2):
        place[k] = places[k]
    pick[...] = jnp.concatenate(places + [jnp.zeros((96, 128), f32)], axis=0).T
    local_mobility[...] = jnp.sqrt(local_mobility[...])
    sub = lax.broadcasted_iota(jnp.int32, (8, 256), 0)
    sums = []
    for c in range(CHUNKS):
        copies[c].wait()
        for v in range(c * step, (c + 1) * step):
            half = (weighted[v].astype(f32) * local_mobility[v : v + 1, :]).astype(bf16)
            weighted[v] = half
            half = half.T
            turned[v] = half
            square = half.astype(f32)
            square = square * square
            total = square[:8]
            for i in range(1, 16):
                total = total + square[8 * i : 8 * i + 8]
            total = jnp.sum(total, axis=0, keepdims=True)
            if v % GROUP == 0:
                sums.append(jnp.broadcast_to(total, (8, 256)))
            else:
                sums[-1] = jnp.where(sub == v % GROUP, total, sums[-1])
    sums = jnp.concatenate(sums, axis=0)
    total = scatter(places, [sums[:, :128], sums[:, 128:]])
    own[:8, :] = total[:8]
    own[8:, :] = jnp.concatenate([local_rhs[...], jnp.zeros((8 - here, 128), f32)], axis=0)
    up[...] = total[8:]


def assemble_tail(tiles, couples, mobility, rhs, weighted, turned, place, pick, own, up, *scratch):
    @pl.when(is_tail())
    def _():
        assemble_here(
            tiles, couples, mobility, rhs, weighted, turned, place, pick, own, up, *scratch
        )

    @pl.when(jnp.logical_not(is_tail()))
    def _():
        up[...] = jnp.zeros_like(up)


def assemble_others(tiles, couples, mobility, rhs, tail_own, tail_up,
                    weighted, turned, place, pick, own, up, swapped, *scratch):
    @pl.when(jnp.logical_not(is_tail()))
    def _():
        assemble_here(
            tiles, couples, mobility, rhs, weighted, turned, place, pick, own, up, *scratch
        )
        odd = position() % 2 == ODD
        swapped[:8, :] = jnp.where(odd, own[:8, :], up[...])
        swapped[8:, :] = own[8:, :]

    @pl.when(is_tail())
    def _():
        own[...] = jnp.zeros_like(own)
        up[...] = jnp.zeros_like(up)
        swapped[...] = tail_own[...]


def keep_head(block, out):
    out[...] = jnp.where(is_head(), block[...], 0.0)


def keep_inner(kept, block, out):
    out[...] = jnp.where(is_head(), kept[...], block[...])


def multiply(weighted, turned, place, pick, mine, following):
    count = weighted.shape[0]
    high, low = parts(jnp.concatenate([mine, following], axis=0))
    none = jnp.zeros_like(high)
    table = jnp.concatenate(
        [
            jnp.concatenate([high, none, low, none], axis=1),
            jnp.concatenate([none, high, none, low], axis=1),
        ],
        axis=0,
    ).astype(bf16)
    values = jnp.dot(pick[:count, :32].astype(bf16), table, preferred_element_type=f32)
    sub = lax.broadcasted_iota(jnp.int32, (8, 128), 0)
    sub2 = lax.broadcasted_iota(jnp.int32, (8, 256), 0)
    inner, outer = [], []
    for g in range(count // GROUP):
        block = values[GROUP * g : GROUP * (g + 1)]
        left = jnp.concatenate([block[:, :256], block[:, 256:]], axis=0).astype(bf16)
        total = None
        for j in range(0, GROUP, 2):
            v = GROUP * g + j
            right = jnp.concatenate([weighted[v], weighted[v + 1]], axis=1)
            both = jnp.dot(left, right, preferred_element_type=f32)
            both = both[:8] + both[8:]
            total = both[:, :128] if total is None else jnp.where(sub == j, both[:, :128], total)
            total = jnp.where(sub == j + 1, both[:, 128:], total)
        inner.append(total)
    for g in range(count // GROUP):
        left = jnp.concatenate(parts(inner[g]), axis=0).astype(bf16)
        total = None
        for j in range(GROUP):
            both = jnp.dot(left, turned[GROUP * g + j], preferred_element_type=f32)
            both = both[:8] + both[8:]
            total = both if total is None else jnp.where(sub2 == j, both, total)
        outer.append(total)
    outer = jnp.concatenate(outer, axis=0)
    total = scatter(place, [outer[:, :128], outer[:, 128:]])
    return total[:8], total[8:]


def starts(here, own, up, from_prev, from_next):
    live = lax.broadcasted_iota(jnp.int32, (8, 128), 0) < here
    other = live & jnp.logical_not(is_last())
    diag = jnp.where(live, own[:8, :] + from_prev[:8, :], 1.0)
    diag_next = jnp.where(other, from_next[:8, :] + up[...], 1.0)
    target = jnp.where(live, own[8:, :], 0.0)
    target_next = jnp.where(other, from_next[8:, :], 0.0)
    scale, scale_next = relax / diag, relax / diag_next
    return scale, target, scale * target, scale_next, target_next, scale_next * target_next


def first_sweep_at(here, known, from_prev, from_next, y_own, y_up, state):
    *matrix, own, up = known
    now = starts(here, own, up, from_prev, from_next)
    y_own[...], y_up[...] = multiply(*matrix, now[2], now[5])
    for i in range(6):
        state[i] = now[i]


def second_sweep_at(matrix, y_own, y_up, state, y_prev, y_next, z_up, rest, factor):
    scale, target, p, scale_next, target_next, p_next = [state[i] for i in range(6)]
    p = p + scale * (target - (y_own[...] + y_prev[...]))
    p_next = p_next + scale_next * (target_next - (y_next[...] + y_up[...]))
    p_next = jnp.where(is_last(), 0.0, p_next)
    z_own, z_up[...] = multiply(*matrix, p, p_next)
    rest[...] = p + scale * (target - z_own)
    factor[...] = scale


def first_even(here, *refs):
    known, (from_prev, from_next), outs = refs[:6], refs[6:8], refs[-3:]

    @pl.when(position() % 2 == EVEN)
    def _():
        first_sweep_at(here, known, from_prev, from_next, *outs)

    @pl.when(position() % 2 == ODD)
    def _():
        outs[0][...] = outs[1][...] = jnp.zeros_like(outs[1])


def first_odd(here, *refs):
    tail, others, (from_prev, from_next), outs = refs[:6], refs[6:12], refs[12:14], refs[-3:]

    @pl.when(is_tail())
    def _():
        first_sweep_at(here, tail, from_prev, from_next, *outs)

    @pl.when((position() % 2 == ODD) & jnp.logical_not(is_tail()))
    def _():
        first_sweep_at(here, others, from_prev, from_next, *outs)

    @pl.when(position() % 2 == EVEN)
    def _():
        outs[0][...] = outs[1][...] = jnp.zeros_like(outs[1])


def second_odd(*refs):
    tail, others, values, outs = refs[:4], refs[4:8], [refs[i] for i in (8, 9, 10, 12, 11)], refs[-3:]

    @pl.when(is_tail())
    def _():
        second_sweep_at(tail, *values, *outs)

    @pl.when((position() % 2 == ODD) & jnp.logical_not(is_tail()))
    def _():
        second_sweep_at(others, *values, *outs)

    @pl.when(position() % 2 == EVEN)
    def _():
        outs[0][...] = jnp.zeros_like(outs[0])


def second_even(*refs):
    matrix, values, outs = refs[:4], refs[4:9], refs[-3:]

    @pl.when(position() % 2 == EVEN)
    def _():
        second_sweep_at(matrix, *values, *outs)

    @pl.when(position() % 2 == ODD)
    def _():
        outs[0][...] = jnp.zeros_like(outs[0])


def finish_even(rest, factor, z_prev, out):
    out[...] = rest[...] - factor[...] * z_prev[...]


def finish(even, rest, factor, z_prev, out):
    odd = rest[...] - factor[...] * z_prev[...]
    out[...] = jnp.where(position() % 2 == ODD, odd, even[...])[: out.shape[0]]


def move(block, route):
    assert sorted(route.values()) == list(range(lax.axis_size("sfc")))
    return lax.ppermute(block, "sfc", list(route.items()))


def opening(block):
    n, size = lax.axis_size("sfc"), plane_size()
    path = [0, 1, size - 2, size - 3, size - 4, size - 1]
    back = 2
    if size == 32:
        path = [0, 1, 8, 9, 16, 17, 24, 25, 26, 27, 30, 29, 28, 31]
        back = 10
    route = {i: i ^ 1 for i in range(n)}
    for first in range(0, n, size):
        for a, b in zip(path, path[1:]):
            route[first + a] = first + b
        route[first + size - 1] = first + size
        route[first + back + 1] = first - size + back
    route[n - 1], route[back + 1] = n - size + back, 0
    return move(block, route)


def inside(block):
    n, size = lax.axis_size("sfc"), plane_size()
    steps = [size - 1, size - 3, size - 4, 0]
    if size == 32:
        steps = [31, 29, 28, 27, 26, 25, 24, 17, 16, 9, 8, 0]
    route = {i: i + 1 for i in range(n)}
    for first in range(0, n, size):
        for a, b in zip(steps[::2], steps[1::2]):
            route[first + a] = first + b
    return move(block, route)


def to_next():
    n, size = lax.axis_size("sfc"), plane_size()
    stops = list(range(4, n, size))
    route = {i: i + 1 for i in range(n)}
    route.update(zip(stops + [n - 1], [0] + [i + 1 for i in stops]))
    return route


def forward(block):
    return move(block, to_next())


def backward(block):
    route = {b: a for a, b in to_next().items()}
    for first in range(0, len(route), plane_size()):
        route[first + 1], route[first + 3] = route[first + 3], route[first + 1]
    return move(block, route)


def swap(block):
    return lax.ppermute(block, "sfc", [(i, i ^ 1) for i in range(lax.axis_size("sfc"))])


def shards(b_tiles, pressure_tile, mobility, rhs):
    count, pairs, size = b_tiles.shape[:3]
    here = rhs.shape[0]
    in_hbm = lambda a: pltpu.with_memory_space_constraint(a, pltpu.HBM)
    in_vmem = lambda a: pltpu.with_memory_space_constraint(a, pltpu.VMEM)
    tiles = b_tiles.reshape(count, pairs * size, size)
    args = tuple(in_hbm(a) for a in (tiles, pressure_tile.T, mobility, rhs))
    small = jax.ShapeDtypeStruct((8, size), f32)
    assembled = (
        pltpu.VMEM(tiles.shape, bf16),
        pltpu.VMEM((count, size, pairs * size), bf16),
        jax.ShapeDtypeStruct((2, 16, 128), f32),
        jax.ShapeDtypeStruct((128, 128), f32),
        jax.ShapeDtypeStruct((16, size), f32),
        small,
    )
    scratch = [
        pltpu.VMEM((pairs, count), jnp.int32),
        pltpu.VMEM((count, size), f32),
        pltpu.VMEM((here, size), f32),
        pltpu.SemaphoreType.DMA((CHUNKS + 3,)),
    ]

    def call(kernel, outs, name, *operands, **more):
        return pl.pallas_call(
            kernel,
            out_shape=outs,
            in_specs=[VMEM] * len(operands),
            out_specs=jax.tree.map(lambda _: VMEM, outs),
            compiler_params=params,
            cost_estimate=cost,
            name=name,
            **more,
        )(*operands)

    def assembled_by(kernel, outs, name, *order):
        weighted, turned, *others = pl.pallas_call(
            kernel,
            out_shape=outs,
            in_specs=[ANY] * 4 + [VMEM] * len(order),
            out_specs=(VMEM,) * len(outs),
            scratch_shapes=scratch,
            compiler_params=params,
            cost_estimate=cost,
            name=name,
        )(*args, *order)
        return in_vmem(weighted), in_vmem(turned), *others

    *tail, own_t, up_t = assembled_by(assemble_tail, assembled, "assemble_tail")
    kept = opening(up_t)
    *others, own, up, swapped = assembled_by(
        assemble_others, assembled + assembled[4:5], "assemble_others", own_t, up_t
    )
    from_next_o = backward(own)
    inner, swapped = inside(up), swap(swapped)
    kept = call(keep_head, small, "keep_head", kept)
    from_prev_e = call(keep_inner, small, "keep_inner", kept, inner)
    first = (small, small, jax.ShapeDtypeStruct((6, 8, size), f32))
    sweep_e = call(
        functools.partial(first_even, here), first, "first_even",
        *others, own, up, from_prev_e, swapped,
    )
    y_next_o, y_prev_o = backward(sweep_e[0]), swap(sweep_e[1])
    sweep_o = call(
        functools.partial(first_odd, here), first, "first_odd",
        *tail, own_t, up_t, *others, own, up, swapped, from_next_o, sweep_e[1],
    )
    y_prev_e, y_next_e = forward(sweep_o[1]), swap(sweep_o[0])
    z_up_o, rest_o, factor_o = call(
        second_odd, (small,) * 3, "second_odd", *tail, *others, *sweep_o, y_next_o, y_prev_o
    )
    z_prev_e = forward(z_up_o)
    z_up_e, rest_e, factor_e = call(
        second_even, (small,) * 3, "second_even", *others, *sweep_e, y_prev_e, y_next_e, z_up_o
    )
    z_prev_o = swap(z_up_e)
    even = call(finish_even, small, "finish_even", rest_e, factor_e, z_prev_e)
    outs = jax.ShapeDtypeStruct(rhs.shape, f32)
    return call(finish, outs, "finish", even, rest_o, factor_o, z_prev_o)


def solution(mesh):
    placed = (P("sfc", None, None, None), P("sfc", None), P("sfc", None), P("sfc", None))
    return jax.shard_map(
        shards, mesh=mesh, in_specs=placed, out_specs=P("sfc", None), check_vma=False
    )
```

```python
import functools

import jax
import jax.numpy as jnp
from jax import lax
from jax.experimental import pallas as pl
from jax.experimental.pallas import tpu as pltpu
from jax.sharding import PartitionSpec as P

relax = 0.5
f32, bf16 = jnp.float32, jnp.bfloat16
UP = 8
CHUNKS = 6
GROUP = 8
ODD, EVEN = 1, 0
cost = pl.CostEstimate(flops=10**10, bytes_accessed=10**8, transcendentals=0)
quick = pl.CostEstimate(flops=0, bytes_accessed=0, transcendentals=0)
VMEM = pl.BlockSpec(memory_space=pltpu.VMEM)
ANY = pl.BlockSpec(memory_space=pl.ANY)
params = pltpu.CompilerParams(vmem_limit_bytes=32 * 1024 * 1024)


def position():
    return lax.axis_index("sfc")


def is_last():
    return position() == lax.axis_size("sfc") - 1


def plane_size():
    return max(lax.axis_size("sfc") // 8, 8)


def is_tail():
    size = plane_size()
    return (position() % size == size - 1) & jnp.logical_not(is_last())


def is_head():
    return position() % plane_size() == 0


def parts(values):
    high = values.astype(bf16).astype(f32)
    return high, values - high


def scatter(place, per_tile):
    total = None
    for k in range(2):
        high, rest = parts(per_tile[k])
        middle, low = parts(rest)
        wide = jnp.concatenate([high, middle, low], axis=1).astype(bf16)
        sums = jnp.dot(
            place[k][:, : wide.shape[0]].astype(bf16), wide, preferred_element_type=f32
        )
        size = sums.shape[1] // 3
        sums = sums[:, :size] + sums[:, size : 2 * size] + sums[:, 2 * size :]
        total = sums if total is None else total + sums
    return total


def assemble_here(tiles, couples, mobility, rhs, weighted, turned, place, pick, own, up,
                  local_couples, local_mobility, local_rhs, sems):
    count, here = tiles.shape[0], rhs.shape[0]
    step = count // CHUNKS
    small = (couples, local_couples), (mobility, local_mobility), (rhs, local_rhs)
    small = [pltpu.make_async_copy(a, b, sems.at[CHUNKS + i]) for i, (a, b) in enumerate(small)]
    for copy in small:
        copy.start()
    copies = []
    for c in range(CHUNKS):
        part = pl.ds(c * step, step)
        copies.append(pltpu.make_async_copy(tiles.at[part], weighted.at[part], sems.at[c]))
        copies[-1].start()
    for copy in small:
        copy.wait()
    slot = local_couples[...] - position() * here
    slot = jnp.where(slot >= here, slot - here + UP, slot)
    rows = lax.broadcasted_iota(jnp.int32, (16, count), 0)
    places = [
        jnp.concatenate(
            [(rows == slot[k : k + 1]).astype(f32), jnp.zeros((16, 128 - count), f32)], axis=1
        )
        for k in range(2)
    ]
    for k in range(2):
        place[k] = places[k]
    pick[...] = jnp.concatenate(places + [jnp.zeros((96, 128), f32)], axis=0).T
    local_mobility[...] = jnp.sqrt(local_mobility[...])
    sub = lax.broadcasted_iota(jnp.int32, (8, 256), 0)
    sums = []
    for c in range(CHUNKS):
        copies[c].wait()
        for v in range(c * step, (c + 1) * step):
            half = (weighted[v].astype(f32) * local_mobility[v : v + 1, :]).astype(bf16)
            weighted[v] = half
            half = half.T
            turned[v] = half
            square = half.astype(f32)
            square = square * square
            total = square[:8]
            for i in range(1, 16):
                total = total + square[8 * i : 8 * i + 8]
            total = jnp.sum(total, axis=0, keepdims=True)
            if v % GROUP == 0:
                sums.append(jnp.broadcast_to(total, (8, 256)))
            else:
                sums[-1] = jnp.where(sub == v % GROUP, total, sums[-1])
    sums = jnp.concatenate(sums, axis=0)
    total = scatter(places, [sums[:, :128], sums[:, 128:]])
    own[:8, :] = total[:8]
    own[8:, :] = jnp.concatenate([local_rhs[...], jnp.zeros((8 - here, 128), f32)], axis=0)
    up[...] = total[8:]


def join(here, couples, weighted, joint, total):
    size = weighted.shape[2]
    total[...] = jnp.zeros_like(total)
    first = position() * here
    for v in range(weighted.shape[0]):
        k = jnp.where(couples[0, v] - first == v % here, 0, 1)
        slot = couples[1 - k, v] - first - here
        slot = jnp.where(slot >= 0, slot, here)
        mine = weighted[v, pl.ds(pl.multiple_of(k * size, size), size), :]
        other = weighted[v, pl.ds(pl.multiple_of((1 - k) * size, size), size), :]
        both = lax.dot_general(
            jnp.concatenate([mine, other], axis=0), other, (((1,), (1,)), ((), ())),
            preferred_element_type=f32,
        )
        total[v % here, slot] += both[:size]
        total[here, slot] += both[size:]
    for row in range(here + 1):
        for column in range(here):
            block = total[row, column]
            high = block.astype(bf16)
            place = pl.ds(row * size, size), pl.ds(column * size, size)
            joint[0, *place] = high
            joint[1, *place] = (block - high.astype(f32)).astype(bf16)


def across(here, joint, mine, following):
    size = mine.shape[1]

    def wide(values):
        both = parts(values)
        return [
            jnp.concatenate([jnp.broadcast_to(x[r : r + 1], (8, size)) for x in both], axis=0)
            for r in range(here)
        ]

    left = jnp.concatenate(wide(mine), axis=1).astype(bf16)
    total = jnp.dot(left, joint[0, : here * size], preferred_element_type=f32)
    total = total + jnp.dot(left, joint[1, : here * size], preferred_element_type=f32)
    sub = lax.broadcasted_iota(jnp.int32, (8, size), 0)
    result = jnp.zeros((8, size), f32)
    for r, left in enumerate(wide(following)):
        block = total[:, r * size : (r + 1) * size]
        for part in range(2):
            right = joint[part, here * size :, r * size : (r + 1) * size]
            block = block + jnp.dot(left.astype(bf16), right, preferred_element_type=f32)
        result = jnp.where(sub == r, block[:8] + block[8:], result)
    return result


def assemble_tail(tiles, couples, mobility, rhs, weighted, turned, place, pick, own, up, *scratch):
    @pl.when(is_tail())
    def _():
        assemble_here(
            tiles, couples, mobility, rhs, weighted, turned, place, pick, own, up, *scratch
        )

    @pl.when(jnp.logical_not(is_tail()))
    def _():
        up[...] = jnp.zeros_like(up)


def assemble_others(tiles, couples, mobility, rhs, tail_own, tail_up,
                    weighted, turned, place, pick, own, up, swapped, joint, *scratch):
    *scratch, total, slots, sem = scratch
    copy = pltpu.make_async_copy(couples, slots, sem)

    @pl.when(is_head())
    def _():
        copy.start()

    @pl.when(jnp.logical_not(is_tail()))
    def _():
        assemble_here(
            tiles, couples, mobility, rhs, weighted, turned, place, pick, own, up, *scratch
        )
        odd = position() % 2 == ODD
        swapped[:8, :] = jnp.where(odd, own[:8, :], up[...])
        swapped[8:, :] = own[8:, :]

    @pl.when(is_head())
    def _():
        copy.wait()
        join(rhs.shape[0], slots, weighted, joint, total)

    @pl.when(is_tail())
    def _():
        own[...] = jnp.zeros_like(own)
        up[...] = jnp.zeros_like(up)
        swapped[...] = tail_own[...]


def keep_head(block, out):
    out[...] = jnp.where(is_head(), block[...], 0.0)


def keep_inner(kept, block, out):
    out[...] = jnp.where(is_head(), kept[...], block[...])


def multiply(weighted, turned, place, pick, mine, following):
    count = weighted.shape[0]
    high, low = parts(jnp.concatenate([mine, following], axis=0))
    none = jnp.zeros_like(high)
    table = jnp.concatenate(
        [
            jnp.concatenate([high, none, low, none], axis=1),
            jnp.concatenate([none, high, none, low], axis=1),
        ],
        axis=0,
    ).astype(bf16)
    values = jnp.dot(pick[:count, :32].astype(bf16), table, preferred_element_type=f32)
    sub = lax.broadcasted_iota(jnp.int32, (8, 128), 0)
    sub2 = lax.broadcasted_iota(jnp.int32, (8, 256), 0)
    inner, outer = [], []
    for g in range(count // GROUP):
        block = values[GROUP * g : GROUP * (g + 1)]
        left = jnp.concatenate([block[:, :256], block[:, 256:]], axis=0).astype(bf16)
        total = None
        for j in range(0, GROUP, 2):
            v = GROUP * g + j
            right = jnp.concatenate([weighted[v], weighted[v + 1]], axis=1)
            both = jnp.dot(left, right, preferred_element_type=f32)
            both = both[:8] + both[8:]
            total = both[:, :128] if total is None else jnp.where(sub == j, both[:, :128], total)
            total = jnp.where(sub == j + 1, both[:, 128:], total)
        inner.append(total)
    for g in range(count // GROUP):
        left = jnp.concatenate(parts(inner[g]), axis=0).astype(bf16)
        total = None
        for j in range(GROUP):
            both = jnp.dot(left, turned[GROUP * g + j], preferred_element_type=f32)
            both = both[:8] + both[8:]
            total = both if total is None else jnp.where(sub2 == j, both, total)
        outer.append(total)
    outer = jnp.concatenate(outer, axis=0)
    total = scatter(place, [outer[:, :128], outer[:, 128:]])
    return total[:8], total[8:]


def starts(here, own, up, from_prev, from_next):
    live = lax.broadcasted_iota(jnp.int32, (8, 128), 0) < here
    other = live & jnp.logical_not(is_last())
    diag = jnp.where(live, own[:8, :] + from_prev[:8, :], 1.0)
    diag_next = jnp.where(other, from_next[:8, :] + up[...], 1.0)
    target = jnp.where(live, own[8:, :], 0.0)
    target_next = jnp.where(other, from_next[8:, :], 0.0)
    scale, scale_next = relax / diag, relax / diag_next
    return scale, target, scale * target, scale_next, target_next, scale_next * target_next


def first_sweep_at(here, known, from_prev, from_next, y_own, y_up, state):
    *matrix, own, up = known
    now = starts(here, own, up, from_prev, from_next)
    y_own[...], y_up[...] = multiply(*matrix, now[2], now[5])
    for i in range(6):
        state[i] = now[i]


def second_values(y_own, y_up, state, y_prev, y_next):
    scale, target, p, scale_next, target_next, p_next = [state[i] for i in range(6)]
    p = p + scale * (target - (y_own[...] + y_prev[...]))
    p_next = p_next + scale_next * (target_next - (y_next[...] + y_up[...]))
    return p, jnp.where(is_last(), 0.0, p_next), scale, target


def second_sweep_at(matrix, values, z_up, rest, factor):
    p, p_next, scale, target = second_values(*values)
    z_own, z_up[...] = multiply(*matrix, p, p_next)
    rest[...] = p + scale * (target - z_own)
    factor[...] = scale


def first_even(here, *refs):
    known, (from_prev, from_next), outs = refs[:6], refs[6:8], refs[-3:]

    @pl.when(position() % 2 == EVEN)
    def _():
        first_sweep_at(here, known, from_prev, from_next, *outs)

    @pl.when(position() % 2 == ODD)
    def _():
        outs[0][...] = outs[1][...] = jnp.zeros_like(outs[1])


def first_odd(here, *refs):
    tail, others, (from_prev, from_next), outs = refs[:6], refs[6:12], refs[12:14], refs[-3:]

    @pl.when(is_tail())
    def _():
        first_sweep_at(here, tail, from_prev, from_next, *outs)

    @pl.when((position() % 2 == ODD) & jnp.logical_not(is_tail()))
    def _():
        first_sweep_at(here, others, from_prev, from_next, *outs)

    @pl.when(position() % 2 == EVEN)
    def _():
        outs[0][...] = outs[1][...] = jnp.zeros_like(outs[1])


def second_odd(*refs):
    tail, others, values, outs = refs[:4], refs[4:8], [refs[i] for i in (8, 9, 10, 12, 11)], refs[-3:]

    @pl.when(is_tail())
    def _():
        second_sweep_at(tail, values, *outs)

    @pl.when((position() % 2 == ODD) & jnp.logical_not(is_tail()))
    def _():
        second_sweep_at(others, values, *outs)

    @pl.when(position() % 2 == EVEN)
    def _():
        outs[0][...] = jnp.zeros_like(outs[0])


def second_even(here, *refs):
    matrix, values, joint, outs = refs[:4], refs[4:9], refs[9], refs[-5:]
    z_up, rest, factor, values_own, values_next = outs

    @pl.when(is_head())
    def _():
        p, p_next, scale, target = second_values(*values)
        z_up[...] = across(here, joint, p, p_next)
        rest[...] = p + scale * target
        factor[...] = scale
        values_own[...] = p
        values_next[...] = p_next

    @pl.when((position() % 2 == EVEN) & jnp.logical_not(is_head()))
    def _():
        second_sweep_at(matrix, values, z_up, rest, factor)

    @pl.when(position() % 2 == ODD)
    def _():
        z_up[...] = jnp.zeros_like(z_up)


def second_late(*refs):
    matrix, (rest, factor, values_own, values_next, out) = refs[:4], refs[4:]

    @pl.when(is_head())
    def _():
        z_own = multiply(*matrix, values_own[...], values_next[...])[0]
        out[...] = rest[...] - factor[...] * z_own

    @pl.when(jnp.logical_not(is_head()))
    def _():
        out[...] = rest[...]


def finish_even(rest, factor, z_prev, out, local, sem):
    @pl.when(position() % 2 == EVEN)
    def _():
        finish_here(rest, factor, z_prev, out, local, sem)


def finish_odd(even, rest, factor, z_prev, out, local, sem):
    @pl.when(position() % 2 == ODD)
    def _():
        finish_here(rest, factor, z_prev, out, local, sem)


def finish_here(rest, factor, z_prev, out, local, sem):
    local[...] = (rest[...] - factor[...] * z_prev[...])[: local.shape[0]]
    copy = pltpu.make_async_copy(local, out, sem)
    copy.start()
    copy.wait()


def move(block, route):
    assert sorted(route.values()) == list(range(lax.axis_size("sfc")))
    return lax.ppermute(block, "sfc", list(route.items()))


def opening(block):
    n, size = lax.axis_size("sfc"), plane_size()
    path = [0, 1, size - 2, size - 3, size - 4, size - 1]
    back = 2
    if size == 32:
        path = [0, 1, 8, 9, 16, 17, 24, 25, 26, 27, 30, 29, 28, 31]
        back = 10
    route = {i: i ^ 1 for i in range(n)}
    for first in range(0, n, size):
        for a, b in zip(path, path[1:]):
            route[first + a] = first + b
        route[first + size - 1] = first + size
        route[first + back + 1] = first - size + back
    route[n - 1], route[back + 1] = n - size + back, 0
    return move(block, route)


def inside(block):
    n, size = lax.axis_size("sfc"), plane_size()
    steps = [size - 1, size - 3, size - 4, 0]
    if size == 32:
        steps = [31, 29, 28, 27, 26, 25, 24, 17, 16, 9, 8, 0]
    route = {i: i + 1 for i in range(n)}
    for first in range(0, n, size):
        for a, b in zip(steps[::2], steps[1::2]):
            route[first + a] = first + b
    return move(block, route)


def to_next():
    n, size = lax.axis_size("sfc"), plane_size()
    stops = list(range(4, n, size))
    route = {i: i + 1 for i in range(n)}
    route.update(zip(stops + [n - 1], [0] + [i + 1 for i in stops]))
    return route


def forward(block):
    return move(block, to_next())


def backward(block):
    route = {b: a for a, b in to_next().items()}
    for first in range(0, len(route), plane_size()):
        route[first + 1], route[first + 3] = route[first + 3], route[first + 1]
    return move(block, route)


def swap(block):
    return lax.ppermute(block, "sfc", [(i, i ^ 1) for i in range(lax.axis_size("sfc"))])


def shards(b_tiles, pressure_tile, mobility, rhs):
    count, pairs, size = b_tiles.shape[:3]
    here = rhs.shape[0]
    in_hbm = lambda a: pltpu.with_memory_space_constraint(a, pltpu.HBM)
    in_vmem = lambda a: pltpu.with_memory_space_constraint(a, pltpu.VMEM)
    tiles = b_tiles.reshape(count, pairs * size, size)
    args = tuple(in_hbm(a) for a in (tiles, pressure_tile.T, mobility, rhs))
    small = jax.ShapeDtypeStruct((8, size), f32)
    assembled = (
        pltpu.VMEM(tiles.shape, bf16),
        pltpu.VMEM((count, size, pairs * size), bf16),
        jax.ShapeDtypeStruct((2, 16, 128), f32),
        jax.ShapeDtypeStruct((128, 128), f32),
        jax.ShapeDtypeStruct((16, size), f32),
        small,
    )
    scratch = [
        pltpu.VMEM((pairs, count), jnp.int32),
        pltpu.VMEM((count, size), f32),
        pltpu.VMEM((here, size), f32),
        pltpu.SemaphoreType.DMA((CHUNKS + 3,)),
    ]

    def call(kernel, outs, name, *operands, cost=cost):
        return pl.pallas_call(
            kernel,
            out_shape=outs,
            in_specs=[VMEM] * len(operands),
            out_specs=jax.tree.map(lambda _: VMEM, outs),
            compiler_params=params,
            cost_estimate=cost,
            name=name,
        )(*operands)

    def assembled_by(kernel, outs, name, *order, more=()):
        weighted, turned, *others = pl.pallas_call(
            kernel,
            out_shape=outs,
            in_specs=[ANY] * 4 + [VMEM] * len(order),
            out_specs=(VMEM,) * len(outs),
            scratch_shapes=scratch + list(more),
            compiler_params=params,
            cost_estimate=cost,
            name=name,
        )(*args, *order)
        return in_vmem(weighted), in_vmem(turned), *others

    *tail, own_t, up_t = assembled_by(assemble_tail, assembled, "assemble_tail")
    kept = opening(up_t)
    joined = pltpu.VMEM((2, (here + 1) * size, here * size), bf16)
    more = (
        pltpu.VMEM((here + 1, here + 1, size, size), f32),
        pltpu.SMEM((pairs, count), jnp.int32),
        pltpu.SemaphoreType.DMA,
    )
    *others, own, up, swapped, joint = assembled_by(
        assemble_others, assembled + (assembled[4], joined), "assemble_others", own_t, up_t, more=more
    )
    joint = in_vmem(joint)
    from_next_o = backward(own)
    inner, swapped = inside(up), swap(swapped)
    kept = call(keep_head, small, "keep_head", kept)
    from_prev_e = call(keep_inner, small, "keep_inner", kept, inner)
    first = (small, small, jax.ShapeDtypeStruct((6, 8, size), f32))
    sweep_e = call(
        functools.partial(first_even, here), first, "first_even",
        *others, own, up, from_prev_e, swapped,
    )
    y_next_o, y_prev_o = backward(sweep_e[0]), swap(sweep_e[1])
    sweep_o = call(
        functools.partial(first_odd, here), first, "first_odd",
        *tail, own_t, up_t, *others, own, up, swapped, from_next_o, sweep_e[1],
    )
    y_prev_e, y_next_e = forward(sweep_o[1]), swap(sweep_o[0])
    z_up_o, rest_o, factor_o = call(
        second_odd, (small,) * 3, "second_odd", *tail, *others, *sweep_o, y_next_o, y_prev_o
    )
    z_prev_e = forward(z_up_o)
    z_up_e, rest_e, factor_e, *values_e = call(
        functools.partial(second_even, here), (small,) * 5, "second_even",
        *others, *sweep_e, y_prev_e, y_next_e, joint, z_up_o, cost=quick,
    )
    z_prev_o = swap(z_up_e)
    rest_e = call(
        second_late, small, "second_late", *others, rest_e, factor_e, *values_e, cost=quick
    )
    last = dict(
        out_shape=jax.ShapeDtypeStruct(rhs.shape, f32),
        out_specs=ANY,
        scratch_shapes=[pltpu.VMEM(rhs.shape, f32), pltpu.SemaphoreType.DMA],
        compiler_params=params,
    )
    even = pl.pallas_call(
        finish_even, in_specs=[VMEM] * 3, cost_estimate=quick, name="finish_even", **last
    )(rest_e, factor_e, z_prev_e)
    return pl.pallas_call(
        finish_odd, in_specs=[ANY] + [VMEM] * 3, input_output_aliases={0: 0}, name="finish_odd", **last
    )(even, rest_o, factor_o, z_prev_o)


def solution(mesh):
    placed = (P("sfc", None, None, None), P("sfc", None), P("sfc", None), P("sfc", None))
    return jax.shard_map(
        shards, mesh=mesh, in_specs=placed, out_specs=P("sfc", None), check_vma=False
    )
```

```python
import functools

import jax
import jax.numpy as jnp
from jax import lax
from jax.experimental import pallas as pl
from jax.experimental.pallas import tpu as pltpu
from jax.sharding import PartitionSpec as P

relax = 0.5
f32, bf16 = jnp.float32, jnp.bfloat16
UP = 8
CHUNKS = 6
GROUP = 8
ODD, EVEN = 1, 0
cost = pl.CostEstimate(flops=10**10, bytes_accessed=10**8, transcendentals=0)
VMEM = pl.BlockSpec(memory_space=pltpu.VMEM)
ANY = pl.BlockSpec(memory_space=pl.ANY)
params = pltpu.CompilerParams(vmem_limit_bytes=32 * 1024 * 1024)


def position():
    return lax.axis_index("sfc")


def is_last():
    return position() == lax.axis_size("sfc") - 1


def plane_size():
    return max(lax.axis_size("sfc") // 8, 8)


def is_tail():
    size = plane_size()
    return (position() % size == size - 1) & jnp.logical_not(is_last())


def is_head():
    return position() % plane_size() == 0


def parts(values):
    high = values.astype(bf16).astype(f32)
    return high, values - high


def scatter(place, per_tile):
    total = None
    for k in range(2):
        high, rest = parts(per_tile[k])
        middle, low = parts(rest)
        wide = jnp.concatenate([high, middle, low], axis=1).astype(bf16)
        sums = jnp.dot(
            place[k][:, : wide.shape[0]].astype(bf16), wide, preferred_element_type=f32
        )
        size = sums.shape[1] // 3
        sums = sums[:, :size] + sums[:, size : 2 * size] + sums[:, 2 * size :]
        total = sums if total is None else total + sums
    return total


def assemble_here(tiles, couples, mobility, rhs, weighted, turned, place, pick, own, up,
                  local_couples, local_mobility, local_rhs, sems):
    count, here = tiles.shape[0], rhs.shape[0]
    step = count // CHUNKS
    small = (couples, local_couples), (mobility, local_mobility), (rhs, local_rhs)
    small = [pltpu.make_async_copy(a, b, sems.at[CHUNKS + i]) for i, (a, b) in enumerate(small)]
    for copy in small:
        copy.start()
    copies = []
    for c in range(CHUNKS):
        part = pl.ds(c * step, step)
        copies.append(pltpu.make_async_copy(tiles.at[part], weighted.at[part], sems.at[c]))
        copies[-1].start()
    for copy in small:
        copy.wait()
    slot = local_couples[...] - position() * here
    slot = jnp.where(slot >= here, slot - here + UP, slot)
    rows = lax.broadcasted_iota(jnp.int32, (16, count), 0)
    places = [
        jnp.concatenate(
            [(rows == slot[k : k + 1]).astype(f32), jnp.zeros((16, 128 - count), f32)], axis=1
        )
        for k in range(2)
    ]
    for k in range(2):
        place[k] = places[k]
    pick[...] = jnp.concatenate(places + [jnp.zeros((96, 128), f32)], axis=0).T
    local_mobility[...] = jnp.sqrt(local_mobility[...])
    sub = lax.broadcasted_iota(jnp.int32, (8, 256), 0)
    sums = []
    for c in range(CHUNKS):
        copies[c].wait()
        for v in range(c * step, (c + 1) * step):
            half = (weighted[v].astype(f32) * local_mobility[v : v + 1, :]).astype(bf16)
            weighted[v] = half
            half = half.T
            turned[v] = half
            square = half.astype(f32)
            square = square * square
            total = square[:8]
            for i in range(1, 16):
                total = total + square[8 * i : 8 * i + 8]
            total = jnp.sum(total, axis=0, keepdims=True)
            if v % GROUP == 0:
                sums.append(jnp.broadcast_to(total, (8, 256)))
            else:
                sums[-1] = jnp.where(sub == v % GROUP, total, sums[-1])
    sums = jnp.concatenate(sums, axis=0)
    total = scatter(places, [sums[:, :128], sums[:, 128:]])
    own[:8, :] = total[:8]
    own[8:, :] = jnp.concatenate([local_rhs[...], jnp.zeros((8 - here, 128), f32)], axis=0)
    up[...] = total[8:]


def join(here, couples, weighted, joint, total):
    size = weighted.shape[2]
    total[...] = jnp.zeros_like(total)
    first = position() * here
    for v in range(weighted.shape[0]):
        k = jnp.where(couples[0, v] - first == v % here, 0, 1)
        slot = couples[1 - k, v] - first - here
        slot = jnp.where(slot >= 0, slot, here)
        mine = weighted[v, pl.ds(pl.multiple_of(k * size, size), size), :]
        other = weighted[v, pl.ds(pl.multiple_of((1 - k) * size, size), size), :]
        both = lax.dot_general(
            jnp.concatenate([mine, other], axis=0), other, (((1,), (1,)), ((), ())),
            preferred_element_type=f32,
        )
        total[v % here, slot] += both[:size]
        total[here, slot] += both[size:]
    for row in range(here + 1):
        for column in range(here):
            block = total[row, column]
            high = block.astype(bf16)
            place = pl.ds(row * size, size), pl.ds(column * size, size)
            joint[0, *place] = high
            joint[1, *place] = (block - high.astype(f32)).astype(bf16)


def across(here, joint, mine, following):
    size = mine.shape[1]

    def wide(values):
        both = parts(values)
        return [
            jnp.concatenate([jnp.broadcast_to(x[r : r + 1], (8, size)) for x in both], axis=0)
            for r in range(here)
        ]

    left = jnp.concatenate(wide(mine), axis=1).astype(bf16)
    total = jnp.dot(left, joint[0, : here * size], preferred_element_type=f32)
    total = total + jnp.dot(left, joint[1, : here * size], preferred_element_type=f32)
    sub = lax.broadcasted_iota(jnp.int32, (8, size), 0)
    result = jnp.zeros((8, size), f32)
    for r, left in enumerate(wide(following)):
        block = total[:, r * size : (r + 1) * size]
        for part in range(2):
            right = joint[part, here * size :, r * size : (r + 1) * size]
            block = block + jnp.dot(left.astype(bf16), right, preferred_element_type=f32)
        result = jnp.where(sub == r, block[:8] + block[8:], result)
    return result


def assemble_tail(tiles, couples, mobility, rhs, weighted, turned, place, pick, own, up, *scratch):
    @pl.when(is_tail())
    def _():
        assemble_here(
            tiles, couples, mobility, rhs, weighted, turned, place, pick, own, up, *scratch
        )

    @pl.when(jnp.logical_not(is_tail()))
    def _():
        up[...] = jnp.zeros_like(up)


def assemble_others(tiles, couples, mobility, rhs, tail_own, tail_up,
                    weighted, turned, place, pick, own, up, swapped, joint, *scratch):
    *scratch, total, slots, sem = scratch
    copy = pltpu.make_async_copy(couples, slots, sem)

    @pl.when(is_head())
    def _():
        copy.start()

    @pl.when(jnp.logical_not(is_tail()))
    def _():
        assemble_here(
            tiles, couples, mobility, rhs, weighted, turned, place, pick, own, up, *scratch
        )
        odd = position() % 2 == ODD
        swapped[:8, :] = jnp.where(odd, own[:8, :], up[...])
        swapped[8:, :] = own[8:, :]

    @pl.when(is_head())
    def _():
        copy.wait()
        join(rhs.shape[0], slots, weighted, joint, total)

    @pl.when(is_tail())
    def _():
        own[...] = jnp.zeros_like(own)
        up[...] = jnp.zeros_like(up)
        swapped[...] = tail_own[...]


def join_tail(here, couples, weighted, order, joint, total, slots, sem):
    @pl.when(is_tail())
    def _():
        copy = pltpu.make_async_copy(couples, slots, sem)
        copy.start()
        copy.wait()
        join(here, slots, weighted, joint, total)


def keep_head(block, out):
    out[...] = jnp.where(is_head(), block[...], 0.0)


def keep_inner(kept, block, out):
    out[...] = jnp.where(is_head(), kept[...], block[...])


def multiply(weighted, turned, place, pick, mine, following):
    count = weighted.shape[0]
    high, low = parts(jnp.concatenate([mine, following], axis=0))
    none = jnp.zeros_like(high)
    table = jnp.concatenate(
        [
            jnp.concatenate([high, none, low, none], axis=1),
            jnp.concatenate([none, high, none, low], axis=1),
        ],
        axis=0,
    ).astype(bf16)
    values = jnp.dot(pick[:count, :32].astype(bf16), table, preferred_element_type=f32)
    sub = lax.broadcasted_iota(jnp.int32, (8, 128), 0)
    sub2 = lax.broadcasted_iota(jnp.int32, (8, 256), 0)
    inner, outer = [], []
    for g in range(count // GROUP):
        block = values[GROUP * g : GROUP * (g + 1)]
        left = jnp.concatenate([block[:, :256], block[:, 256:]], axis=0).astype(bf16)
        total = None
        for j in range(0, GROUP, 2):
            v = GROUP * g + j
            right = jnp.concatenate([weighted[v], weighted[v + 1]], axis=1)
            both = jnp.dot(left, right, preferred_element_type=f32)
            both = both[:8] + both[8:]
            total = both[:, :128] if total is None else jnp.where(sub == j, both[:, :128], total)
            total = jnp.where(sub == j + 1, both[:, 128:], total)
        inner.append(total)
    for g in range(count // GROUP):
        left = jnp.concatenate(parts(inner[g]), axis=0).astype(bf16)
        total = None
        for j in range(GROUP):
            both = jnp.dot(left, turned[GROUP * g + j], preferred_element_type=f32)
            both = both[:8] + both[8:]
            total = both if total is None else jnp.where(sub2 == j, both, total)
        outer.append(total)
    outer = jnp.concatenate(outer, axis=0)
    total = scatter(place, [outer[:, :128], outer[:, 128:]])
    return total[:8], total[8:]


def starts(here, own, up, from_prev, from_next):
    live = lax.broadcasted_iota(jnp.int32, (8, 128), 0) < here
    other = live & jnp.logical_not(is_last())
    diag = jnp.where(live, own[:8, :] + from_prev[:8, :], 1.0)
    diag_next = jnp.where(other, from_next[:8, :] + up[...], 1.0)
    target = jnp.where(live, own[8:, :], 0.0)
    target_next = jnp.where(other, from_next[8:, :], 0.0)
    scale, scale_next = relax / diag, relax / diag_next
    return scale, target, scale * target, scale_next, target_next, scale_next * target_next


def first_sweep_at(here, known, from_prev, from_next, y_own, y_up, state):
    *matrix, own, up = known
    now = starts(here, own, up, from_prev, from_next)
    y_own[...], y_up[...] = multiply(*matrix, now[2], now[5])
    for i in range(6):
        state[i] = now[i]


def second_values(y_own, y_up, state, y_prev, y_next):
    scale, target, p, scale_next, target_next, p_next = [state[i] for i in range(6)]
    p = p + scale * (target - (y_own[...] + y_prev[...]))
    p_next = p_next + scale_next * (target_next - (y_next[...] + y_up[...]))
    return p, jnp.where(is_last(), 0.0, p_next), scale, target


def second_sweep_at(matrix, values, z_up, rest, factor):
    p, p_next, scale, target = second_values(*values)
    z_own, z_up[...] = multiply(*matrix, p, p_next)
    rest[...] = p + scale * (target - z_own)
    factor[...] = scale


def first_even(here, *refs):
    known, (from_prev, from_next), outs = refs[:6], refs[6:8], refs[-3:]

    @pl.when(position() % 2 == EVEN)
    def _():
        first_sweep_at(here, known, from_prev, from_next, *outs)

    @pl.when(position() % 2 == ODD)
    def _():
        outs[0][...] = outs[1][...] = jnp.zeros_like(outs[1])


def first_odd(here, *refs):
    tail, others, (from_prev, from_next, joint), outs = refs[:6], refs[6:12], refs[12:15], refs[-3:]
    y_own, y_up, state = outs

    @pl.when(is_tail())
    def _():
        now = starts(here, *tail[4:], from_prev, from_next)
        y_up[...] = across(here, joint, now[2], now[5])
        y_own[...] = jnp.zeros_like(y_own)
        for i in range(6):
            state[i] = now[i]

    @pl.when((position() % 2 == ODD) & jnp.logical_not(is_tail()))
    def _():
        first_sweep_at(here, others, from_prev, from_next, *outs)

    @pl.when(position() % 2 == EVEN)
    def _():
        y_own[...] = y_up[...] = jnp.zeros_like(y_up)


def first_late(*refs):
    matrix, (y_own, state, _, out) = refs[:4], refs[4:]

    @pl.when(is_tail())
    def _():
        out[...] = multiply(*matrix, state[2], state[5])[0]

    @pl.when(jnp.logical_not(is_tail()))
    def _():
        out[...] = y_own[...]


def second_urgent(here, values, joint, z_up, rest, factor, values_own, values_next):
    p, p_next, scale, target = second_values(*values)
    z_up[...] = across(here, joint, p, p_next)
    rest[...] = p + scale * target
    factor[...] = scale
    values_own[...] = p
    values_next[...] = p_next


def second_odd(here, *refs):
    others, values, joint, outs = refs[:4], [refs[i] for i in (4, 5, 6, 8, 7)], refs[9], refs[-5:]

    @pl.when(is_tail())
    def _():
        second_urgent(here, values, joint, *outs)

    @pl.when((position() % 2 == ODD) & jnp.logical_not(is_tail()))
    def _():
        second_sweep_at(others, values, *outs[:3])

    @pl.when(position() % 2 == EVEN)
    def _():
        outs[0][...] = jnp.zeros_like(outs[0])


def second_even(here, *refs):
    matrix, values, joint, outs = refs[:4], refs[4:9], refs[9], refs[-5:]

    @pl.when(is_head())
    def _():
        second_urgent(here, values, joint, *outs)

    @pl.when((position() % 2 == EVEN) & jnp.logical_not(is_head()))
    def _():
        second_sweep_at(matrix, values, *outs[:3])

    @pl.when(position() % 2 == ODD)
    def _():
        outs[0][...] = jnp.zeros_like(outs[0])


def second_late(role, *refs):
    matrix, (rest, factor, values_own, values_next, out) = refs[:4], refs[4:]

    @pl.when(role())
    def _():
        z_own = multiply(*matrix, values_own[...], values_next[...])[0]
        out[...] = rest[...] - factor[...] * z_own

    @pl.when(jnp.logical_not(role()))
    def _():
        out[...] = rest[...]


def finish_even(rest, factor, z_prev, out, local, sem):
    @pl.when(position() % 2 == EVEN)
    def _():
        finish_here(rest, factor, z_prev, out, local, sem)


def finish_odd(even, rest, factor, z_prev, out, local, sem):
    @pl.when(position() % 2 == ODD)
    def _():
        finish_here(rest, factor, z_prev, out, local, sem)


def finish_here(rest, factor, z_prev, out, local, sem):
    local[...] = (rest[...] - factor[...] * z_prev[...])[: local.shape[0]]
    copy = pltpu.make_async_copy(local, out, sem)
    copy.start()
    copy.wait()


def move(block, route):
    assert sorted(route.values()) == list(range(lax.axis_size("sfc")))
    return lax.ppermute(block, "sfc", list(route.items()))


def opening(block):
    n, size = lax.axis_size("sfc"), plane_size()
    path = [0, 1, size - 2, size - 3, size - 4, size - 1]
    back = 2
    if size == 32:
        path = [0, 1, 8, 9, 16, 17, 24, 25, 26, 27, 30, 29, 28, 31]
        back = 10
    route = {i: i ^ 1 for i in range(n)}
    for first in range(0, n, size):
        for a, b in zip(path, path[1:]):
            route[first + a] = first + b
        route[first + size - 1] = first + size
        route[first + back + 1] = first - size + back
    route[n - 1], route[back + 1] = n - size + back, 0
    return move(block, route)


def inside(block):
    n, size = lax.axis_size("sfc"), plane_size()
    steps = [size - 1, size - 3, size - 4, 0]
    if size == 32:
        steps = [31, 29, 28, 27, 26, 25, 24, 17, 16, 9, 8, 0]
    route = {i: i + 1 for i in range(n)}
    for first in range(0, n, size):
        for a, b in zip(steps[::2], steps[1::2]):
            route[first + a] = first + b
    return move(block, route)


def to_next():
    n, size = lax.axis_size("sfc"), plane_size()
    stops = list(range(4, n, size))
    route = {i: i + 1 for i in range(n)}
    route.update(zip(stops + [n - 1], [0] + [i + 1 for i in stops]))
    return route


def forward(block):
    return move(block, to_next())


def backward(block):
    route = {b: a for a, b in to_next().items()}
    for first in range(0, len(route), plane_size()):
        route[first + 1], route[first + 3] = route[first + 3], route[first + 1]
    return move(block, route)


def swap(block):
    return lax.ppermute(block, "sfc", [(i, i ^ 1) for i in range(lax.axis_size("sfc"))])


def shards(b_tiles, pressure_tile, mobility, rhs):
    count, pairs, size = b_tiles.shape[:3]
    here = rhs.shape[0]
    in_hbm = lambda a: pltpu.with_memory_space_constraint(a, pltpu.HBM)
    in_vmem = lambda a: pltpu.with_memory_space_constraint(a, pltpu.VMEM)
    tiles = b_tiles.reshape(count, pairs * size, size)
    args = tuple(in_hbm(a) for a in (tiles, pressure_tile.T, mobility, rhs))
    small = jax.ShapeDtypeStruct((8, size), f32)
    assembled = (
        pltpu.VMEM(tiles.shape, bf16),
        pltpu.VMEM((count, size, pairs * size), bf16),
        jax.ShapeDtypeStruct((2, 16, 128), f32),
        jax.ShapeDtypeStruct((128, 128), f32),
        jax.ShapeDtypeStruct((16, size), f32),
        small,
    )
    scratch = [
        pltpu.VMEM((pairs, count), jnp.int32),
        pltpu.VMEM((count, size), f32),
        pltpu.VMEM((here, size), f32),
        pltpu.SemaphoreType.DMA((CHUNKS + 3,)),
    ]

    def call(kernel, outs, name, *operands):
        return pl.pallas_call(
            kernel,
            out_shape=outs,
            in_specs=[VMEM] * len(operands),
            out_specs=jax.tree.map(lambda _: VMEM, outs),
            compiler_params=params,
            cost_estimate=cost,
            name=name,
        )(*operands)

    def assembled_by(kernel, outs, name, *order, more=()):
        weighted, turned, *others = pl.pallas_call(
            kernel,
            out_shape=outs,
            in_specs=[ANY] * 4 + [VMEM] * len(order),
            out_specs=(VMEM,) * len(outs),
            scratch_shapes=scratch + list(more),
            compiler_params=params,
            cost_estimate=cost,
            name=name,
        )(*args, *order)
        return in_vmem(weighted), in_vmem(turned), *others

    *tail, own_t, up_t = assembled_by(assemble_tail, assembled, "assemble_tail")
    kept = opening(up_t)
    joined = pltpu.VMEM((2, (here + 1) * size, here * size), bf16)
    more = (
        pltpu.VMEM((here + 1, here + 1, size, size), f32),
        pltpu.SMEM((pairs, count), jnp.int32),
        pltpu.SemaphoreType.DMA,
    )
    *others, own, up, swapped, joint = assembled_by(
        assemble_others, assembled + (assembled[4], joined), "assemble_others", own_t, up_t, more=more
    )
    joint = in_vmem(joint)
    from_next_o = backward(own)
    inner, swapped = inside(up), swap(swapped)
    kept = call(keep_head, small, "keep_head", kept)
    from_prev_e = call(keep_inner, small, "keep_inner", kept, inner)
    first = (small, small, jax.ShapeDtypeStruct((6, 8, size), f32))
    sweep_e = call(
        functools.partial(first_even, here), first, "first_even",
        *others, own, up, from_prev_e, swapped,
    )
    y_next_o, y_prev_o = backward(sweep_e[0]), swap(sweep_e[1])
    joint_t = in_vmem(
        pl.pallas_call(
            functools.partial(join_tail, here),
            out_shape=joined,
            in_specs=[ANY, VMEM, VMEM],
            out_specs=VMEM,
            scratch_shapes=more,
            compiler_params=params,
            cost_estimate=cost,
            name="join_tail",
        )(args[1], tail[0], sweep_e[0])
    )
    y_own_o, y_up_o, state_o = call(
        functools.partial(first_odd, here), first, "first_odd",
        *tail, own_t, up_t, *others, own, up, swapped, from_next_o, joint_t, sweep_e[1],
    )
    y_own_o = call(first_late, small, "first_late", *tail, y_own_o, state_o, state_o)
    sweep_o = y_own_o, y_up_o, state_o
    y_prev_e, y_next_e = forward(sweep_o[1]), swap(sweep_o[0])
    z_up_o, rest_o, factor_o, *values_o = call(
        functools.partial(second_odd, here), (small,) * 5, "second_odd",
        *others, *sweep_o, y_next_o, y_prev_o, joint_t,
    )
    z_prev_e = forward(z_up_o)
    z_up_e, rest_e, factor_e, *values_e = call(
        functools.partial(second_even, here), (small,) * 5, "second_even",
        *others, *sweep_e, y_prev_e, y_next_e, joint, z_up_o,
    )
    z_prev_o = swap(z_up_e)
    rest_e = call(
        functools.partial(second_late, is_head), small, "late_even",
        *others, rest_e, factor_e, *values_e,
    )
    rest_o = call(
        functools.partial(second_late, is_tail), small, "late_odd",
        *tail, rest_o, factor_o, *values_o,
    )
    last = dict(
        out_shape=jax.ShapeDtypeStruct(rhs.shape, f32),
        out_specs=ANY,
        scratch_shapes=[pltpu.VMEM(rhs.shape, f32), pltpu.SemaphoreType.DMA],
        compiler_params=params,
    )
    even = pl.pallas_call(
        finish_even, in_specs=[VMEM] * 3, name="finish_even", **last
    )(rest_e, factor_e, z_prev_e)
    return pl.pallas_call(
        finish_odd, in_specs=[ANY] + [VMEM] * 3, input_output_aliases={0: 0}, name="finish_odd", **last
    )(even, rest_o, factor_o, z_prev_o)


def solution(mesh):
    placed = (P("sfc", None, None, None), P("sfc", None), P("sfc", None), P("sfc", None))
    return jax.shard_map(
        shards, mesh=mesh, in_specs=placed, out_specs=P("sfc", None), check_vma=False
    )
```

```python
import functools

import jax
import jax.numpy as jnp
from jax import lax
from jax.experimental import pallas as pl
from jax.experimental.pallas import tpu as pltpu
from jax.sharding import PartitionSpec as P

relax = 0.5
f32, bf16 = jnp.float32, jnp.bfloat16
UP = 8
CHUNKS = 4
GROUP = 8
ODD, EVEN = 1, 0
cost = pl.CostEstimate(flops=10**10, bytes_accessed=10**8, transcendentals=0)
VMEM = pl.BlockSpec(memory_space=pltpu.VMEM)
ANY = pl.BlockSpec(memory_space=pl.ANY)
params = pltpu.CompilerParams(vmem_limit_bytes=32 * 1024 * 1024)


def position():
    return lax.axis_index("sfc")


def is_last():
    return position() == lax.axis_size("sfc") - 1


def plane_size():
    return max(lax.axis_size("sfc") // 8, 8)


def is_tail():
    size = plane_size()
    return (position() % size == size - 1) & jnp.logical_not(is_last())


def is_head():
    return position() % plane_size() == 0


def parts(values):
    high = values.astype(bf16).astype(f32)
    return high, values - high


def scatter(place, per_tile):
    total = None
    for k in range(2):
        high, rest = parts(per_tile[k])
        middle, low = parts(rest)
        wide = jnp.concatenate([high, middle, low], axis=1).astype(bf16)
        sums = jnp.dot(
            place[k][:, : wide.shape[0]].astype(bf16), wide, preferred_element_type=f32
        )
        size = sums.shape[1] // 3
        sums = sums[:, :size] + sums[:, size : 2 * size] + sums[:, 2 * size :]
        total = sums if total is None else total + sums
    return total


def assemble_here(tiles, couples, mobility, rhs, weighted, turned, place, pick, own, up,
                  local_couples, local_mobility, local_rhs, sems):
    count, here = tiles.shape[0], rhs.shape[0]
    step = count // CHUNKS
    small = (couples, local_couples), (mobility, local_mobility), (rhs, local_rhs)
    small = [pltpu.make_async_copy(a, b, sems.at[CHUNKS + i]) for i, (a, b) in enumerate(small)]
    for copy in small:
        copy.start()
    copies = []
    for c in range(CHUNKS):
        part = pl.ds(c * step, step)
        copies.append(pltpu.make_async_copy(tiles.at[part], weighted.at[part], sems.at[c]))
        copies[-1].start()
    for copy in small:
        copy.wait()
    slot = local_couples[...] - position() * here
    slot = jnp.where(slot >= here, slot - here + UP, slot)
    rows = lax.broadcasted_iota(jnp.int32, (16, count), 0)
    places = [
        jnp.concatenate(
            [(rows == slot[k : k + 1]).astype(f32), jnp.zeros((16, 128 - count), f32)], axis=1
        )
        for k in range(2)
    ]
    for k in range(2):
        place[k] = places[k]
    pick[...] = jnp.concatenate(places + [jnp.zeros((96, 128), f32)], axis=0).T
    local_mobility[...] = jnp.sqrt(local_mobility[...])
    sub = lax.broadcasted_iota(jnp.int32, (8, 256), 0)
    sums = []
    for c in range(CHUNKS):
        copies[c].wait()
        for v in range(c * step, (c + 1) * step):
            half = (weighted[v].astype(f32) * local_mobility[v : v + 1, :]).astype(bf16)
            weighted[v] = half
            half = half.T
            turned[v] = half
            square = half.astype(f32)
            square = square * square
            total = square[:8]
            for i in range(1, 16):
                total = total + square[8 * i : 8 * i + 8]
            total = jnp.sum(total, axis=0, keepdims=True)
            if v % GROUP == 0:
                sums.append(jnp.broadcast_to(total, (8, 256)))
            else:
                sums[-1] = jnp.where(sub == v % GROUP, total, sums[-1])
    sums = jnp.concatenate(sums, axis=0)
    total = scatter(places, [sums[:, :128], sums[:, 128:]])
    own[:8, :] = total[:8]
    own[8:, :] = jnp.concatenate([local_rhs[...], jnp.zeros((8 - here, 128), f32)], axis=0)
    up[...] = total[8:]


def join(here, couples, weighted, joint, total):
    size = weighted.shape[2]
    total[...] = jnp.zeros_like(total)
    first = position() * here
    for v in range(weighted.shape[0]):
        k = jnp.where(couples[0, v] - first == v % here, 0, 1)
        slot = couples[1 - k, v] - first - here
        slot = jnp.where(slot >= 0, slot, here)
        mine = weighted[v, pl.ds(pl.multiple_of(k * size, size), size), :]
        other = weighted[v, pl.ds(pl.multiple_of((1 - k) * size, size), size), :]
        both = lax.dot_general(
            jnp.concatenate([mine, other], axis=0), other, (((1,), (1,)), ((), ())),
            preferred_element_type=f32,
        )
        total[v % here, slot] += both[:size]
        total[here, slot] += both[size:]
    for row in range(here + 1):
        for column in range(here):
            block = total[row, column]
            high = block.astype(bf16)
            place = pl.ds(row * size, size), pl.ds(column * size, size)
            joint[0, *place] = high
            joint[1, *place] = (block - high.astype(f32)).astype(bf16)


def across(here, joint, mine, following):
    size = mine.shape[1]

    def wide(values):
        both = parts(values)
        return [
            jnp.concatenate([jnp.broadcast_to(x[r : r + 1], (8, size)) for x in both], axis=0)
            for r in range(here)
        ]

    left = jnp.concatenate(wide(mine), axis=1).astype(bf16)
    total = jnp.dot(left, joint[0, : here * size], preferred_element_type=f32)
    total = total + jnp.dot(left, joint[1, : here * size], preferred_element_type=f32)
    sub = lax.broadcasted_iota(jnp.int32, (8, size), 0)
    result = jnp.zeros((8, size), f32)
    for r, left in enumerate(wide(following)):
        block = total[:, r * size : (r + 1) * size]
        for part in range(2):
            right = joint[part, here * size :, r * size : (r + 1) * size]
            block = block + jnp.dot(left.astype(bf16), right, preferred_element_type=f32)
        result = jnp.where(sub == r, block[:8] + block[8:], result)
    return result


def assemble_tail(tiles, couples, mobility, rhs, weighted, turned, place, pick, own, up, *scratch):
    @pl.when(is_tail())
    def _():
        assemble_here(
            tiles, couples, mobility, rhs, weighted, turned, place, pick, own, up, *scratch
        )

    @pl.when(jnp.logical_not(is_tail()))
    def _():
        up[...] = jnp.zeros_like(up)


def assemble_others(tiles, couples, mobility, rhs, tail_own, tail_up,
                    weighted, turned, place, pick, own, up, swapped, joint, *scratch):
    *scratch, total, slots, sem = scratch
    copy = pltpu.make_async_copy(couples, slots, sem)

    @pl.when(is_head())
    def _():
        copy.start()

    @pl.when(jnp.logical_not(is_tail()))
    def _():
        assemble_here(
            tiles, couples, mobility, rhs, weighted, turned, place, pick, own, up, *scratch
        )
        odd = position() % 2 == ODD
        swapped[:8, :] = jnp.where(odd, own[:8, :], up[...])
        swapped[8:, :] = own[8:, :]

    @pl.when(is_head())
    def _():
        copy.wait()
        join(rhs.shape[0], slots, weighted, joint, total)

    @pl.when(is_tail())
    def _():
        own[...] = jnp.zeros_like(own)
        up[...] = jnp.zeros_like(up)
        swapped[...] = tail_own[...]


def join_tail(here, couples, weighted, order, joint, total, slots, sem):
    @pl.when(is_tail())
    def _():
        copy = pltpu.make_async_copy(couples, slots, sem)
        copy.start()
        copy.wait()
        join(here, slots, weighted, joint, total)


def keep_head(block, out):
    out[...] = jnp.where(is_head(), block[...], 0.0)


def keep_inner(kept, block, out):
    out[...] = jnp.where(is_head(), kept[...], block[...])


def scatter_at_once(place, per_tile):
    count, size = per_tile[0].shape
    wide = jnp.concatenate(parts(jnp.concatenate(per_tile, axis=0)), axis=1).astype(bf16)
    left = jnp.concatenate([place[k][:, :count] for k in range(2)], axis=1).astype(bf16)
    sums = jnp.dot(left, wide, preferred_element_type=f32)
    return sums[:, :size] + sums[:, size:]


def multiply(weighted, turned, place, pick, mine, following):
    count = weighted.shape[0]
    high, low = parts(jnp.concatenate([mine, following], axis=0))
    none = jnp.zeros_like(high)
    table = jnp.concatenate(
        [
            jnp.concatenate([high, none, low, none], axis=1),
            jnp.concatenate([none, high, none, low], axis=1),
        ],
        axis=0,
    ).astype(bf16)
    values = jnp.dot(pick[:count, :32].astype(bf16), table, preferred_element_type=f32)
    sub = lax.broadcasted_iota(jnp.int32, (8, 128), 0)
    sub2 = lax.broadcasted_iota(jnp.int32, (8, 256), 0)
    inner, outer = [], []
    for g in range(count // GROUP):
        block = values[GROUP * g : GROUP * (g + 1)]
        left = jnp.concatenate([block[:, :256], block[:, 256:]], axis=0).astype(bf16)
        total = None
        for j in range(0, GROUP, 2):
            v = GROUP * g + j
            right = jnp.concatenate([weighted[v], weighted[v + 1]], axis=1)
            both = jnp.dot(left, right, preferred_element_type=f32)
            both = both[:8] + both[8:]
            total = both[:, :128] if total is None else jnp.where(sub == j, both[:, :128], total)
            total = jnp.where(sub == j + 1, both[:, 128:], total)
        inner.append(total)
    for g in range(count // GROUP):
        left = jnp.concatenate(parts(inner[g]), axis=0).astype(bf16)
        total = None
        for j in range(GROUP):
            both = jnp.dot(left, turned[GROUP * g + j], preferred_element_type=f32)
            both = both[:8] + both[8:]
            total = both if total is None else jnp.where(sub2 == j, both, total)
        outer.append(total)
    outer = jnp.concatenate(outer, axis=0)
    total = scatter_at_once(place, [outer[:, :128], outer[:, 128:]])
    return total[:8], total[8:]


def starts(here, own, up, from_prev, from_next):
    live = lax.broadcasted_iota(jnp.int32, (8, 128), 0) < here
    other = live & jnp.logical_not(is_last())
    diag = jnp.where(live, own[:8, :] + from_prev[:8, :], 1.0)
    diag_next = jnp.where(other, from_next[:8, :] + up[...], 1.0)
    target = jnp.where(live, own[8:, :], 0.0)
    target_next = jnp.where(other, from_next[8:, :], 0.0)
    scale, scale_next = relax / diag, relax / diag_next
    return scale, target, scale * target, scale_next, target_next, scale_next * target_next


def first_sweep_at(here, known, from_prev, from_next, y_own, y_up, state):
    *matrix, own, up = known
    now = starts(here, own, up, from_prev, from_next)
    y_own[...], y_up[...] = multiply(*matrix, now[2], now[5])
    for i in range(6):
        state[i] = now[i]


def second_values(y_own, y_up, state, y_prev, y_next):
    scale, target, p, scale_next, target_next, p_next = [state[i] for i in range(6)]
    p = p + scale * (target - (y_own[...] + y_prev[...]))
    p_next = p_next + scale_next * (target_next - (y_next[...] + y_up[...]))
    return p, jnp.where(is_last(), 0.0, p_next), scale, target


def second_sweep_at(matrix, values, z_up, rest, factor):
    p, p_next, scale, target = second_values(*values)
    z_own, z_up[...] = multiply(*matrix, p, p_next)
    rest[...] = p + scale * (target - z_own)
    factor[...] = scale


def first_even(here, *refs):
    known, (from_prev, from_next), outs = refs[:6], refs[6:8], refs[-3:]

    @pl.when(position() % 2 == EVEN)
    def _():
        first_sweep_at(here, known, from_prev, from_next, *outs)

    @pl.when(position() % 2 == ODD)
    def _():
        outs[0][...] = outs[1][...] = jnp.zeros_like(outs[1])


def first_odd(here, *refs):
    tail, others, (from_prev, from_next, joint), outs = refs[:6], refs[6:12], refs[12:15], refs[-3:]
    y_own, y_up, state = outs

    @pl.when(is_tail())
    def _():
        now = starts(here, *tail[4:], from_prev, from_next)
        y_up[...] = across(here, joint, now[2], now[5])
        y_own[...] = jnp.zeros_like(y_own)
        for i in range(6):
            state[i] = now[i]

    @pl.when((position() % 2 == ODD) & jnp.logical_not(is_tail()))
    def _():
        first_sweep_at(here, others, from_prev, from_next, *outs)

    @pl.when(position() % 2 == EVEN)
    def _():
        y_own[...] = y_up[...] = jnp.zeros_like(y_up)


def first_late(*refs):
    matrix, (y_own, state, _, out) = refs[:4], refs[4:]

    @pl.when(is_tail())
    def _():
        out[...] = multiply(*matrix, state[2], state[5])[0]

    @pl.when(jnp.logical_not(is_tail()))
    def _():
        out[...] = y_own[...]


def second_urgent(here, values, joint, z_up, rest, factor, values_own, values_next):
    p, p_next, scale, target = second_values(*values)
    z_up[...] = across(here, joint, p, p_next)
    rest[...] = p + scale * target
    factor[...] = scale
    values_own[...] = p
    values_next[...] = p_next


def second_odd(here, *refs):
    others, values, joint, outs = refs[:4], [refs[i] for i in (4, 5, 6, 8, 7)], refs[9], refs[-5:]

    @pl.when(is_tail())
    def _():
        second_urgent(here, values, joint, *outs)

    @pl.when((position() % 2 == ODD) & jnp.logical_not(is_tail()))
    def _():
        second_sweep_at(others, values, *outs[:3])

    @pl.when(position() % 2 == EVEN)
    def _():
        outs[0][...] = jnp.zeros_like(outs[0])


def second_even(here, *refs):
    matrix, values, joint, outs = refs[:4], refs[4:9], refs[9], refs[-5:]

    @pl.when(is_head())
    def _():
        second_urgent(here, values, joint, *outs)

    @pl.when((position() % 2 == EVEN) & jnp.logical_not(is_head()))
    def _():
        second_sweep_at(matrix, values, *outs[:3])

    @pl.when(position() % 2 == ODD)
    def _():
        outs[0][...] = jnp.zeros_like(outs[0])


def second_late(role, *refs):
    matrix, (rest, factor, values_own, values_next, out) = refs[:4], refs[4:]

    @pl.when(role())
    def _():
        z_own = multiply(*matrix, values_own[...], values_next[...])[0]
        out[...] = rest[...] - factor[...] * z_own

    @pl.when(jnp.logical_not(role()))
    def _():
        out[...] = rest[...]


def finish_even(rest, factor, z_prev, out, local, sem):
    @pl.when(position() % 2 == EVEN)
    def _():
        finish_here(rest, factor, z_prev, out, local, sem)


def finish_odd(even, rest, factor, z_prev, out, local, sem):
    @pl.when(position() % 2 == ODD)
    def _():
        finish_here(rest, factor, z_prev, out, local, sem)


def finish_here(rest, factor, z_prev, out, local, sem):
    local[...] = (rest[...] - factor[...] * z_prev[...])[: local.shape[0]]
    copy = pltpu.make_async_copy(local, out, sem)
    copy.start()
    copy.wait()


def move(block, route):
    assert sorted(route.values()) == list(range(lax.axis_size("sfc")))
    return lax.ppermute(block, "sfc", list(route.items()))


def opening(block):
    n, size = lax.axis_size("sfc"), plane_size()
    path = [0, 1, size - 2, size - 3, size - 4, size - 1]
    back = 2
    if size == 32:
        path = [0, 1, 8, 9, 16, 17, 24, 25, 26, 27, 30, 29, 28, 31]
        back = 10
    route = {i: i ^ 1 for i in range(n)}
    for first in range(0, n, size):
        for a, b in zip(path, path[1:]):
            route[first + a] = first + b
        route[first + size - 1] = first + size
        route[first + back + 1] = first - size + back
    route[n - 1], route[back + 1] = n - size + back, 0
    return move(block, route)


def inside(block):
    n, size = lax.axis_size("sfc"), plane_size()
    steps = [size - 1, size - 3, size - 4, 0]
    if size == 32:
        steps = [31, 29, 28, 27, 26, 25, 24, 17, 16, 9, 8, 0]
    route = {i: i + 1 for i in range(n)}
    for first in range(0, n, size):
        for a, b in zip(steps[::2], steps[1::2]):
            route[first + a] = first + b
    return move(block, route)


def to_next():
    n, size = lax.axis_size("sfc"), plane_size()
    stops = list(range(4, n, size))
    route = {i: i + 1 for i in range(n)}
    route.update(zip(stops + [n - 1], [0] + [i + 1 for i in stops]))
    return route


def forward(block):
    return move(block, to_next())


def backward(block):
    route = {b: a for a, b in to_next().items()}
    for first in range(0, len(route), plane_size()):
        route[first + 1], route[first + 3] = route[first + 3], route[first + 1]
    return move(block, route)


def swap(block):
    return lax.ppermute(block, "sfc", [(i, i ^ 1) for i in range(lax.axis_size("sfc"))])


def shards(b_tiles, pressure_tile, mobility, rhs):
    count, pairs, size = b_tiles.shape[:3]
    here = rhs.shape[0]
    in_hbm = lambda a: pltpu.with_memory_space_constraint(a, pltpu.HBM)
    in_vmem = lambda a: pltpu.with_memory_space_constraint(a, pltpu.VMEM)
    tiles = b_tiles.reshape(count, pairs * size, size)
    args = tuple(in_hbm(a) for a in (tiles, pressure_tile.T, mobility, rhs))
    small = jax.ShapeDtypeStruct((8, size), f32)
    assembled = (
        pltpu.VMEM(tiles.shape, bf16),
        pltpu.VMEM((count, size, pairs * size), bf16),
        jax.ShapeDtypeStruct((2, 16, 128), f32),
        jax.ShapeDtypeStruct((128, 128), f32),
        jax.ShapeDtypeStruct((16, size), f32),
        small,
    )
    scratch = [
        pltpu.VMEM((pairs, count), jnp.int32),
        pltpu.VMEM((count, size), f32),
        pltpu.VMEM((here, size), f32),
        pltpu.SemaphoreType.DMA((CHUNKS + 3,)),
    ]

    def call(kernel, outs, name, *operands):
        return pl.pallas_call(
            kernel,
            out_shape=outs,
            in_specs=[VMEM] * len(operands),
            out_specs=jax.tree.map(lambda _: VMEM, outs),
            compiler_params=params,
            cost_estimate=cost,
            name=name,
        )(*operands)

    def assembled_by(kernel, outs, name, *order, more=()):
        weighted, turned, *others = pl.pallas_call(
            kernel,
            out_shape=outs,
            in_specs=[ANY] * 4 + [VMEM] * len(order),
            out_specs=(VMEM,) * len(outs),
            scratch_shapes=scratch + list(more),
            compiler_params=params,
            cost_estimate=cost,
            name=name,
        )(*args, *order)
        return in_vmem(weighted), in_vmem(turned), *others

    *tail, own_t, up_t = assembled_by(assemble_tail, assembled, "assemble_tail")
    kept = opening(up_t)
    joined = pltpu.VMEM((2, (here + 1) * size, here * size), bf16)
    more = (
        pltpu.VMEM((here + 1, here + 1, size, size), f32),
        pltpu.SMEM((pairs, count), jnp.int32),
        pltpu.SemaphoreType.DMA,
    )
    *others, own, up, swapped, joint = assembled_by(
        assemble_others, assembled + (assembled[4], joined), "assemble_others", own_t, up_t, more=more
    )
    joint = in_vmem(joint)
    from_next_o = backward(own)
    inner, swapped = inside(up), swap(swapped)
    kept = call(keep_head, small, "keep_head", kept)
    from_prev_e = call(keep_inner, small, "keep_inner", kept, inner)
    first = (small, small, jax.ShapeDtypeStruct((6, 8, size), f32))
    sweep_e = call(
        functools.partial(first_even, here), first, "first_even",
        *others, own, up, from_prev_e, swapped,
    )
    y_next_o, y_prev_o = backward(sweep_e[0]), swap(sweep_e[1])
    joint_t = in_vmem(
        pl.pallas_call(
            functools.partial(join_tail, here),
            out_shape=joined,
            in_specs=[ANY, VMEM, VMEM],
            out_specs=VMEM,
            scratch_shapes=more,
            compiler_params=params,
            cost_estimate=cost,
            name="join_tail",
        )(args[1], tail[0], sweep_e[0])
    )
    y_own_o, y_up_o, state_o = call(
        functools.partial(first_odd, here), first, "first_odd",
        *tail, own_t, up_t, *others, own, up, swapped, from_next_o, joint_t, sweep_e[1],
    )
    y_own_o = call(first_late, small, "first_late", *tail, y_own_o, state_o, state_o)
    sweep_o = y_own_o, y_up_o, state_o
    y_prev_e, y_next_e = forward(sweep_o[1]), swap(sweep_o[0])
    z_up_o, rest_o, factor_o, *values_o = call(
        functools.partial(second_odd, here), (small,) * 5, "second_odd",
        *others, *sweep_o, y_next_o, y_prev_o, joint_t,
    )
    z_prev_e = forward(z_up_o)
    z_up_e, rest_e, factor_e, *values_e = call(
        functools.partial(second_even, here), (small,) * 5, "second_even",
        *others, *sweep_e, y_prev_e, y_next_e, joint, z_up_o,
    )
    z_prev_o = swap(z_up_e)
    rest_e = call(
        functools.partial(second_late, is_head), small, "late_even",
        *others, rest_e, factor_e, *values_e,
    )
    rest_o = call(
        functools.partial(second_late, is_tail), small, "late_odd",
        *tail, rest_o, factor_o, *values_o,
    )
    last = dict(
        out_shape=jax.ShapeDtypeStruct(rhs.shape, f32),
        out_specs=ANY,
        scratch_shapes=[pltpu.VMEM(rhs.shape, f32), pltpu.SemaphoreType.DMA],
        compiler_params=params,
    )
    even = pl.pallas_call(
        finish_even, in_specs=[VMEM] * 3, name="finish_even", **last
    )(rest_e, factor_e, z_prev_e)
    return pl.pallas_call(
        finish_odd, in_specs=[ANY] + [VMEM] * 3, input_output_aliases={0: 0}, name="finish_odd", **last
    )(even, rest_o, factor_o, z_prev_o)


def solution(mesh):
    placed = (P("sfc", None, None, None), P("sfc", None), P("sfc", None), P("sfc", None))
    return jax.shard_map(
        shards, mesh=mesh, in_specs=placed, out_specs=P("sfc", None), check_vma=False
    )
```
